512 devices in a mesh: slab: 16 (over y, x), pencil: 32 (over z, core).
Axes of the slice: x: 4, y: 4, z: 16, core: 2. Of those that a mesh axis runs over, the one named last changes fastest.
Arguments:
- wavefunction: float32 [256, 2, 16, 32, 256], P('pencil', None, None, 'slab'), may hold values from -6 to 6
- propagator: float32 [2, 256, 256], replicated
- lengths: int32 [32, 256], P('slab', 'pencil'), may hold values from 1 to 256, as said below
- centrifugal: float32 [3, 16], replicated, may hold values from 0.5 to 6
- channel_pairs: int32 [32, 2], replicated, may hold values from 0 to 15, as said below
- strengths: float32 [32], replicated, may hold values from 0.5 to 4
Outputs:
- evolved: float32 [256, 2, 16, 32, 256], P('pencil', None, None, 'slab')
The draws below stay inside these ranges and needn't reach their ends.
Inputs may be any that keep to these rules, and one draw needn't show every extreme that they name: `lengths`: every draw has a row with all 256 points live. `channel_pairs`: the two channels of a pair differ; a pair may occur more than once.
All inputs are finite; a program needn't handle non-finite values.
Results may differ from the reference program's by a relative error of at most 0.0001.
Values sent between devices are 32-bit elements; how exact they have to be, the bound alone decides.
A program may use at most 64 MiB of HBM per device.

```python
import math
import jax
import jax.numpy as jnp
from jax import lax

N = 256
C = 16
P_SIZE = 32
NR3 = 32


def draw_propagator(key, part):
    key = jax.random.fold_in(key, 11)
    spread = 0.5 / N ** 0.5
    random_part = jax.random.normal(key, (2, N, N), jnp.float32)
    diagonal = 0.8
    identity = jnp.eye(N, dtype=jnp.float32)
    return random_part * spread + jnp.stack([diagonal * identity, jnp.zeros_like(identity)])


def draw_lengths(key, part):
    key = jax.random.fold_in(key, 23)
    radius_key, jitter_key = jax.random.split(key)
    squared = jax.random.randint(radius_key, (), N * N, N * N + N * N // 4)
    index_three = jnp.arange(NR3, dtype=jnp.int32)
    index_two = jnp.arange(N, dtype=jnp.int32)
    index_one = jnp.arange(N, dtype=jnp.int32)
    radial_sum = index_three[:, None] * index_three[:, None] + index_two[None, :] * index_two[None, :]
    within = jnp.sum((radial_sum[:, :, None] + (index_one * index_one)[None, None, :] < squared).astype(jnp.int32), axis=2)
    jitter = jax.random.randint(jitter_key, (NR3, N), 1, 33)
    return jnp.minimum(within + jitter, N).astype(jnp.int32)


def draw_channel_pairs(key, part):
    key = jax.random.fold_in(key, 37)
    left_key, offset_key = jax.random.split(key)
    left_side = jax.random.randint(left_key, (P_SIZE,), 0, C)
    offsets = jax.random.randint(offset_key, (P_SIZE,), 1, C)
    return jnp.stack([left_side, (left_side + offsets) % C], axis=1).astype(jnp.int32)


def shard_levels(stream_key, shape, pieces, least, largest):
    def one(position, shards_of):
        steps = jax.random.uniform(jax.random.fold_in(jax.random.fold_in(stream_key, 6), position), (shards_of,), jnp.float32, least / len(pieces), largest / len(pieces))
        return jnp.repeat(jnp.exp(steps), shape[position] // shards_of).reshape((-1,) + (1,) * (len(shape) - position - 1))

    level = one(*pieces[0])
    for cut in pieces[1:]:
        level = level * one(*cut)
    return level


def gaussian(key, extent, deviation, bound, cuts=(), kind=jnp.bfloat16):
    result = deviation * jax.random.normal(key, extent, jnp.float32)
    if cuts:
        result = result * shard_levels(key, extent, cuts, -0.22, 0.18)
    return jnp.clip(result, -bound, bound).astype(kind)


def setup_inputs(seed: int = 0) -> dict:
    seeds = jax.random.split(jax.random.key(seed), 7)
    wavefunction = gaussian(seeds[0], (N, 2, C, NR3, N), 1.0, 6.0, ((0, 32), (3, 16)), jnp.float32)
    propagator = draw_propagator(jax.random.fold_in(seeds[6], 71), 0)
    lengths = draw_lengths(jax.random.fold_in(seeds[6], 71), 0)
    centrifugal = jnp.clip(jnp.exp(jax.random.uniform(seeds[3], (3, C), jnp.float32, math.log(0.5), math.log(6.0))), 0.5, 6.0)
    channel_pairs = draw_channel_pairs(jax.random.fold_in(seeds[6], 71), 0)
    strengths = jnp.clip(jnp.exp(jax.random.uniform(seeds[5], (P_SIZE,), jnp.float32, math.log(0.5), math.log(4.0))), 0.5, 4.0)
    return {"wavefunction": wavefunction, "propagator": propagator, "lengths": lengths, "centrifugal": centrifugal, "channel_pairs": channel_pairs, "strengths": strengths}


step_tau = 0.1
grid_step = 0.5
charge = 3.0
band_beta = 0.3
highest = lax.Precision.HIGHEST


def coupling_matrix(channel_pairs, strengths, channels):
    labels = jnp.arange(channels, dtype=jnp.int32)
    first_hot = (channel_pairs[:, 0:1] == labels[None, :]).astype(jnp.float32)
    second_hot = (channel_pairs[:, 1:2] == labels[None, :]).astype(jnp.float32)
    single = jnp.dot((first_hot * strengths[:, None]).T, second_hot, precision=highest)
    return single + single.T


def radial_terms(positions, weights):
    radius = grid_step * (positions.astype(jnp.float32) + 1.0)
    return -charge / radius[None, :] + weights[:, None] / (radius * radius)[None, :]


def block_matrix(propagator):
    upper = jnp.stack([propagator[0], -propagator[1]])
    lower = jnp.stack([propagator[1], propagator[0]])
    return jnp.stack([upper, lower])


def potential_step(current, duration, table, centrifugal, coupling, second_pos, third_pos, first_pos):
    first_terms = radial_terms(first_pos, centrifugal[0])
    second_terms = radial_terms(second_pos, centrifugal[1])
    third_terms = radial_terms(third_pos, centrifugal[2])
    phases = duration * (second_terms.T[:, :, None, None] + third_terms[None, :, :, None] + first_terms[None, :, None, :])
    cosine = jnp.cos(phases)[:, None]
    sine_part = jnp.sin(phases)[:, None]
    swapped = jnp.flip(current, axis=1)
    signs = jnp.array([1.0, -1.0], dtype=jnp.float32)[None, :, None, None, None]
    turned = current * cosine + signs * swapped * sine_part
    farthest = jnp.maximum(jnp.maximum(second_pos[:, None, None], third_pos[None, :, None]), first_pos[None, None, :]).astype(jnp.float32)
    weight = (duration / (1.0 + 0.02 * farthest))[:, None, None]
    live = (first_pos[None, None, :] < table.T[:, :, None]).astype(jnp.float32)[:, None, None]
    mixed = jnp.einsum("cd,xpdyz->xpcyz", coupling, jnp.flip(turned, axis=1), precision=highest)
    return (turned + signs * weight * mixed) * live


def along_last(current, propagator):
    return jnp.einsum("xpcyk,qpjk->xqcyj", current, block_matrix(propagator), precision=highest)


def along_first(current, propagator):
    return jnp.einsum("qpjk,kpcyz->jqcyz", block_matrix(propagator), current, precision=highest)


def band_apply(padded, count):
    def plane(offset):
        return lax.slice_in_dim(padded, offset, offset + count, axis=3)

    return band_beta * (plane(0) - 16.0 * plane(1) + 30.0 * plane(2) - 16.0 * plane(3) + plane(4)) / 24.0


def combine_band(current, first_pass, second_pass):
    signs = jnp.array([1.0, -1.0], dtype=jnp.float32)[None, :, None, None, None]
    return current + signs * jnp.flip(first_pass, axis=1) - 0.5 * second_pass


def radial_band(current):
    count = current.shape[3]
    padding = ((0, 0), (0, 0), (0, 0), (2, 2), (0, 0))
    first_pass = band_apply(jnp.pad(current, padding), count)
    second_pass = band_apply(jnp.pad(first_pass, padding), count)
    return combine_band(current, first_pass, second_pass)


def reference(wavefunction, propagator, lengths, centrifugal, channel_pairs, strengths):
    coupling = coupling_matrix(channel_pairs, strengths, centrifugal.shape[1])
    second_pos = jnp.arange(N, dtype=jnp.int32)
    third_pos = jnp.arange(NR3, dtype=jnp.int32)
    first_pos = jnp.arange(N, dtype=jnp.int32)
    current = potential_step(wavefunction, 0.5 * step_tau, lengths, centrifugal, coupling, second_pos, third_pos, first_pos)
    for sweep in range(2):
        current = along_last(current, propagator)
        current = along_first(current, propagator)
        current = radial_band(current)
        duration = step_tau if sweep == 0 else 0.5 * step_tau
        current = potential_step(current, duration, lengths, centrifugal, coupling, second_pos, third_pos, first_pos)
    return current
```

```python
import jax
import jax.numpy as jnp
from jax import lax
from jax.experimental import pallas as pl
from jax.experimental.pallas import tpu as pltpu
from jax.sharding import PartitionSpec as P


MESH = pl.DeviceIdType.MESH
F32 = jnp.float32
BF16 = jnp.bfloat16
STEP = 0.1
GRID = 0.5
CHARGE = 3.0
BAND = 0.3
NP = 32
NS = 16
L2 = 8
L3 = 2
C = 16
N = 256
CHUNKS = 2


def iota(shape, dim):
    return lax.broadcasted_iota(jnp.int32, shape, dim)


def split2(x):
    high = x.astype(BF16)
    return high, (x - high.astype(F32)).astype(BF16)


def split3(x):
    high = x.astype(BF16)
    rest = x - high.astype(F32)
    middle = rest.astype(BF16)
    return high, middle, (rest - middle.astype(F32)).astype(BF16)


def product(a, b, contract=((1,), (0,))):
    def one(x, y):
        return lax.dot_general(x, y, (contract, ((), ())), preferred_element_type=F32)

    return one(a[0], b[0]) + (one(a[0], b[1]) + one(a[1], b[0]))


def column(row, count):
    shape = (count, row.shape[1])
    return jnp.sum(jnp.where(iota(shape, 0) == iota(shape, 1), row, jnp.zeros_like(row)), axis=1, keepdims=True)


def radial(position, weight):
    radius = GRID * (position.astype(F32) + 1.0)
    return -CHARGE / radius + weight / (radius * radius)


def flip_blocks(x):
    row, group = iota((1, 8, 128), 1), iota((1, 8, 128), 2) // 16
    for bit in (4, 2, 1):
        lanes = 16 * bit
        has_row, has_group = (row // bit) % 2, (group // bit) % 2
        down = pltpu.roll(pltpu.roll(x, bit, 1), 128 - lanes, 2)
        if bit == 4:
            up = down
        else:
            up = pltpu.roll(pltpu.roll(x, 8 - bit, 1), lanes, 2)
        x = jnp.where(has_row == has_group, x, jnp.where(has_row == 1, down, up))
    return x


def band(x):
    zero = jnp.zeros((2,) + x.shape[1:], F32)
    padded = jnp.concatenate([zero, x, zero], axis=0)
    n = x.shape[0]
    outer = padded[0:n] + padded[4 : n + 4]
    inner = padded[1 : n + 1] + padded[3 : n + 3]
    return (BAND / 24.0) * (outer - 16.0 * inner + 30.0 * x)


def body(
    x_ref,
    prop_ref,
    len_ref,
    cent_ref,
    pair_ref,
    str_ref,
    o_ref,
    cos_a,
    sin_a,
    wl_a,
    lv_a,
    kron_hi,
    kron_lo,
    mix_hi,
    mix_lo,
    w1_hi,
    w1_lo,
    q2_hi,
    q2_lo,
    wf_hi,
    wf_lo,
    cos_d,
    sin_d,
    u_hi,
    u_lo,
    len_col,
    len_in,
    len_out,
    ybuf,
    bbuf,
    sbuf,
    dbuf,
    ebuf,
    hbuf,
    gbuf,
    rbuf,
    send_sem,
    recv_sem,
    len_send,
    len_recv,
):
    p = lax.axis_index("pencil")
    s = lax.axis_index("slab")
    barrier = pltpu.get_barrier_semaphore()

    def far(n, size):
        half = (n + 1) // 2
        return size // 2 + (1 - 2 * (n % 2)) * half

    def pencil_peer(n):
        return lax.rem(p + far(n, NP), NP)

    def slab_peer(n):
        return lax.rem(s + far(n, NS), NS)

    @pl.loop(0, NP - 1)
    def _(n):
        pl.semaphore_signal(barrier, inc=1, device_id=(s, pencil_peer(n)), device_id_type=MESH)

    @pl.loop(0, NS - 1)
    def _(n):
        pl.semaphore_signal(barrier, inc=1, device_id=(slab_peer(n), p), device_id_type=MESH)

    def copy(src, dst, k, device):
        return pltpu.make_async_remote_copy(
            src_ref=src,
            dst_ref=dst,
            send_sem=send_sem.at[k],
            recv_sem=recv_sem.at[k],
            device_id=device,
            device_id_type=MESH,
        )

    def pencil_exchange(src, dst, chunk, k):
        @pl.loop(0, NP - 1)
        def _(n):
            q = pencil_peer(n)
            copy(src.at[chunk, q], dst.at[chunk, p], k, (s, q)).start()

        dst[chunk, pl.ds(p, 1)] = src[chunk, pl.ds(p, 1)]

    def slab_exchange(src, dst, chunk, k):
        @pl.loop(0, NS - 1)
        def _(n):
            q = slab_peer(n)
            copy(src.at[chunk, q], dst.at[chunk, s], k, (q, p)).start()

        dst[chunk, pl.ds(s, 1)] = src[chunk, pl.ds(s, 1)]

    def arrived(buf, chunk, k, count):
        part = buf.at[chunk, pl.ds(0, count - 1)]
        copy(part, part, k, (s, p)).wait_recv()

    def left(buf, chunk, k, count):
        part = buf.at[chunk, pl.ds(0, count - 1)]
        copy(part, part, k, (s, p)).wait_send()

    lens = len_ref[...].astype(F32)
    lane = iota((8, 128), 1)
    len_tile = jnp.zeros((8, 128), F32)
    len_rows = []
    for i3 in range(L3):
        col = column(lens[i3 : i3 + 1], L2)
        len_rows.append(col)
        len_tile = len_tile + jnp.where(lane == L3 * s + i3, col, jnp.zeros_like(col))
    len_out[0] = len_tile
    len_a = jnp.concatenate(len_rows, axis=0)

    strength = str_ref[...]
    first, second = pair_ref[0:1, :], pair_ref[1:2, :]

    def hot_rows(labels):
        return (iota((N, 32), 0) % C == labels).astype(F32)

    def hot_cols(labels):
        shape = (32, 32)
        col = jnp.sum(jnp.where(iota(shape, 0) == iota(shape, 1), labels, 0), axis=1, keepdims=True)
        return (iota((32, N), 1) % C == col).astype(F32)

    rows_1, rows_2, cols_1, cols_2 = hot_rows(first), hot_rows(second), hot_cols(first), hot_cols(second)
    tiled = jnp.zeros((N, N), F32)
    for part in split3(strength):
        scale = part.astype(F32)
        tiled = tiled + jnp.dot((rows_1 * scale).astype(BF16), cols_2.astype(BF16), preferred_element_type=F32)
        tiled = tiled + jnp.dot((rows_2 * scale).astype(BF16), cols_1.astype(BF16), preferred_element_type=F32)
    row, col = iota((N, N), 0), iota((N, N), 1)
    kron_hi[...], kron_lo[...] = split2(jnp.where(row // C == col // C, tiled, 0.0))
    row, col = iota((128, 128), 0), iota((128, 128), 1)
    same = (row // C) % 4 == (col // C) % 4
    sign = (row // 64 - col // 64).astype(F32)
    mix_hi[...], mix_lo[...] = split2(jnp.where(same, tiled[:128, :128] * sign, 0.0))

    half = 0.5 * STEP
    cent = cent_ref[...]
    cent_col = [column(cent[e : e + 1], C) for e in range(3)]
    angle_1 = half * radial(iota((C, N), 1), cent_col[0])
    cos_1, sin_1 = jnp.cos(angle_1), jnp.sin(angle_1)
    lane = iota((C, 16), 1)
    angle_23 = half * (radial(L2 * p + lane % L2, cent_col[1]) + radial(L3 * s + lane // L2, cent_col[2]))
    cos_23, sin_23 = jnp.cos(angle_23), jnp.sin(angle_23)
    for m in range(16):
        c23, s23 = cos_23[:, m : m + 1], sin_23[:, m : m + 1]
        cos_a[m * C : (m + 1) * C] = cos_1 * c23 - sin_1 * s23
        sin_a[m * C : (m + 1) * C] = sin_1 * c23 + cos_1 * s23
    row, col = iota((16, N), 0), iota((16, N), 1)
    farthest = jnp.maximum(jnp.maximum(L2 * p + row % L2, L3 * s + row // L2), col).astype(F32)
    live = (col.astype(F32) < len_a).astype(F32)
    lv_a[...] = live
    wl_a[...] = live * (half / (1.0 + 0.02 * farthest))

    sub = iota((1, 8, 2 * N), 1)

    def interleaved(re, im):
        top = jnp.concatenate([re, -im], axis=1).reshape(NP, 8, 2 * N)
        low = jnp.concatenate([im, re], axis=1).reshape(NP, 8, 2 * N)
        early = jnp.where(sub < 4, top, pltpu.roll(low, 4, 1))
        late = jnp.where(sub < 4, pltpu.roll(top, 4, 1), low)
        return [split2(v.reshape(N, 2 * N)) for v in (early, late)]

    for chunk, (high, low) in enumerate(interleaved(prop_ref[0], prop_ref[1])):
        w1_hi[chunk], w1_lo[chunk] = high, low

    kron = (kron_hi[...], kron_lo[...])

    def potential(re, im):
        cosine, sine = cos_a[...], sin_a[...]
        turned_re = re * cosine + im * sine
        turned_im = im * cosine - re * sine
        mixed_re = product(kron, split2(turned_im))
        mixed_im = product(kron, split2(turned_re))

        def rows(a):
            return jnp.concatenate([jnp.broadcast_to(a[m : m + 1], (C, N)) for m in range(16)], axis=0)

        weight, alive = rows(wl_a[...]), rows(lv_a[...])
        return turned_re * alive + weight * mixed_re, turned_im * alive - weight * mixed_im

    def load(part):
        blocks = []
        for i3 in range(L3):
            for i2 in range(L2):
                base = (i2 * 2 + part) * 64 + i3
                blocks.append(
                    jnp.concatenate([x_ref[pl.ds(base + 2 * l, C, stride=4), :] for l in range(2)], axis=1)
                )
        return jnp.concatenate(blocks, axis=0)

    v_re, v_im = potential(load(0), load(1))
    u_hi[...], u_lo[...] = split2(jnp.concatenate([v_re, v_im], axis=1))
    u = (u_hi[...], u_lo[...])

    for chunk in range(CHUNKS):
        y = product((w1_hi[chunk], w1_lo[chunk]), u, ((1,), (1,)))
        for i3 in range(L3):
            ybuf[chunk, :, i3] = y[:, i3 * 128 : (i3 + 1) * 128].reshape(NP, 8, 128)
        if chunk == 0:
            pl.semaphore_wait(barrier, NP + NS - 2)
        pencil_exchange(ybuf, bbuf, chunk, chunk)

    root = s == p // 2

    def len_copy(src, dst, k, device):
        return pltpu.make_async_remote_copy(
            src_ref=src,
            dst_ref=dst,
            send_sem=len_send.at[k],
            recv_sem=len_recv.at[k],
            device_id=device,
            device_id_type=MESH,
        )

    @pl.when(jnp.logical_not(root))
    def _():
        first_copy = len_copy(len_out.at[0], len_col.at[s], 0, (p // 2, p))
        first_copy.start()
        first_copy.wait_send()

    @pl.when(root)
    def _():
        len_col[pl.ds(s, 1)] = len_out[pl.ds(0, 1)]
        part = len_col.at[pl.ds(0, NS - 1)]
        len_copy(part, part, 0, (s, p)).wait_recv()
        total = jnp.sum(len_col[...], axis=0)
        len_out[1] = total
        len_in[pl.ds(lax.rem(p, 2), 1)] = total[None]

        @pl.loop(0, NP - 1)
        def _(n):
            len_copy(len_out.at[1], len_in.at[lax.rem(p, 2)], 1, (s, pencil_peer(n))).start()

        @pl.loop(0, NP - 1)
        def _(n):
            len_copy(len_out.at[1], len_in.at[0], 1, (s, p)).wait_send()

        len_copy(len_in.at[0], len_in.at[0], 1, (s, p)).wait_recv()

    @pl.when(jnp.logical_not(root))
    def _():
        len_copy(len_in, len_in, 1, (s, p)).wait_recv()

    re, im = prop_ref[0], prop_ref[1]
    q2_hi[...], q2_lo[...] = split2(jnp.concatenate([re, im], axis=0))
    for chunk, (high, low) in enumerate(interleaved(re.T, -im.T)):
        wf_hi[chunk], wf_lo[chunk] = high, low

    lane = iota((C, 128), 1)
    cent_row = [
        jnp.sum(jnp.where(iota((C, 128), 0) == lane % C, col, 0.0), axis=0, keepdims=True) for col in cent_col
    ]
    lane = iota((1, 128), 1)
    rows_2 = C * s + iota((16, 128), 0)
    angle_2 = STEP * radial(rows_2, cent_row[1])
    angle_3 = STEP * radial(iota((32, 128), 0), cent_row[2])
    cos_3, sin_3 = jnp.cos(angle_3), jnp.sin(angle_3)
    turn = jnp.where(lane < 64, 1.0, -1.0)
    for chunk in range(CHUNKS):
        angle_12 = angle_2 + STEP * radial(8 * p + 4 * chunk + (lane // C) % 4, cent_row[0])
        cos_12, sin_12 = jnp.cos(angle_12), jnp.sin(angle_12)
        for i3 in range(32):
            c3, s3 = cos_3[i3 : i3 + 1], sin_3[i3 : i3 + 1]
            cos_d[chunk, i3] = cos_12 * c3 - sin_12 * s3
            sin_d[chunk, i3] = turn * (sin_12 * c3 + cos_12 * s3)

    q2 = (q2_hi[...], q2_lo[...])

    def second_line(z):
        both = product(q2, split2(z))
        a, b = both[:N], both[N:]
        lane = iota((1, 128), 1)
        sign = jnp.where(lane < 64, -1.0, 1.0)
        return [
            a[:, i * 128 : (i + 1) * 128] + sign * pltpu.roll(b[:, i * 128 : (i + 1) * 128], 64, 1) for i in range(L3)
        ]

    def third_line(psi):
        g1 = band(psi)
        g2 = band(g1)
        return psi + turn * pltpu.roll(g1, 64, 2) - 0.5 * g2

    def third_potential(psi, chunk):
        turned = psi * cos_d[chunk] + sin_d[chunk] * pltpu.roll(psi, 64, 2)
        mixed = product(split2(turned.reshape(512, 128)), (mix_hi[...], mix_lo[...])).reshape(32, 16, 128)
        first_pos = 8 * p + 4 * chunk + (lane // C) % 4
        both = jnp.maximum(rows_2, first_pos)
        lengths = jnp.concatenate([len_in[0], len_in[1]], axis=0)
        out = []
        for i3 in range(32):
            weight = STEP / (1.0 + 0.02 * jnp.maximum(both, i3).astype(F32))
            alive = first_pos.astype(F32) < lengths[:, i3 : i3 + 1]
            out.append(jnp.where(alive, turned[i3] + weight * mixed[i3], 0.0))
        return jnp.stack(out, axis=0)

    for chunk in range(CHUNKS):
        arrived(bbuf, chunk, chunk, NP)
        z = [flip_blocks(bbuf[chunk, :, i3]).reshape(N, 128) for i3 in range(L3)]
        z = second_line(jnp.concatenate(z, axis=1))
        for i3 in range(L3):
            sbuf[chunk, :, i3] = z[i3].reshape(NS, 16, 128)
        slab_exchange(sbuf, dbuf, chunk, 2 + chunk)

        arrived(dbuf, chunk, 2 + chunk, NS)
        psi = third_line(dbuf[chunk].reshape(32, 16, 128))
        psi = third_line(third_potential(psi, chunk))
        ebuf[chunk] = psi.reshape(NS, L3, 16, 128)
        slab_exchange(ebuf, hbuf, chunk, 4 + chunk)

        arrived(hbuf, chunk, 4 + chunk, NS)
        z = [hbuf[chunk, :, i3].reshape(N, 128) for i3 in range(L3)]
        z = second_line(jnp.concatenate(z, axis=1))
        for i3 in range(L3):
            gbuf[chunk, :, i3] = flip_blocks(z[i3].reshape(NP, 8, 128))
        pencil_exchange(gbuf, rbuf, chunk, 6 + chunk)

    out = jnp.zeros((N, 2 * N), F32)
    for chunk in range(CHUNKS):
        arrived(rbuf, chunk, 6 + chunk, NP)
        r = jnp.concatenate([rbuf[chunk, :, i3].reshape(N, 128) for i3 in range(L3)], axis=1)
        out = out + product(split2(r.T), (wf_hi[chunk], wf_lo[chunk]))

    out = potential(out[:, :N], out[:, N:])
    for part in range(2):
        for i3 in range(L3):
            for i2 in range(L2):
                base = (i2 * 2 + part) * 64 + i3
                start = (i3 * L2 + i2) * C
                for l in range(2):
                    o_ref[pl.ds(base + 2 * l, C, stride=4), :] = out[part][start : start + C, l * 128 : (l + 1) * 128]

    for chunk in range(CHUNKS):
        left(ybuf, chunk, chunk, NP)
        left(sbuf, chunk, 2 + chunk, NS)
        left(ebuf, chunk, 4 + chunk, NS)
        left(gbuf, chunk, 6 + chunk, NP)


def on_device(wavefunction, propagator, lengths, centrifugal, channel_pairs, strengths):
    shape = wavefunction.shape
    x = wavefunction.reshape(8, 2, 16, 2, 2, 128).transpose(0, 1, 2, 4, 3, 5).reshape(1024, 128)

    def vmem(*dims, dtype=F32):
        return pltpu.VMEM(dims, dtype)

    scratch = [
        vmem(N, N),
        vmem(N, N),
        vmem(16, N),
        vmem(16, N),
        vmem(N, N, dtype=BF16),
        vmem(N, N, dtype=BF16),
        vmem(128, 128, dtype=BF16),
        vmem(128, 128, dtype=BF16),
        vmem(CHUNKS, N, 2 * N, dtype=BF16),
        vmem(CHUNKS, N, 2 * N, dtype=BF16),
        vmem(2 * N, N, dtype=BF16),
        vmem(2 * N, N, dtype=BF16),
        vmem(CHUNKS, N, 2 * N, dtype=BF16),
        vmem(CHUNKS, N, 2 * N, dtype=BF16),
        vmem(CHUNKS, 32, 16, 128),
        vmem(CHUNKS, 32, 16, 128),
        vmem(N, 2 * N, dtype=BF16),
        vmem(N, 2 * N, dtype=BF16),
        vmem(NS, 8, 128),
        vmem(2, 8, 128),
        vmem(2, 8, 128),
        vmem(CHUNKS, NP, L3, 8, 128),
        vmem(CHUNKS, NP, L3, 8, 128),
        vmem(CHUNKS, NS, L3, 16, 128),
        vmem(CHUNKS, NS, L3, 16, 128),
        vmem(CHUNKS, NS, L3, 16, 128),
        vmem(CHUNKS, NS, L3, 16, 128),
        vmem(CHUNKS, NP, L3, 8, 128),
        vmem(CHUNKS, NP, L3, 8, 128),
        pltpu.SemaphoreType.DMA((8,)),
        pltpu.SemaphoreType.DMA((8,)),
        pltpu.SemaphoreType.DMA((2,)),
        pltpu.SemaphoreType.DMA((2,)),
    ]
    whole = pl.BlockSpec(memory_space=pltpu.VMEM)
    out = pl.pallas_call(
        body,
        out_shape=jax.ShapeDtypeStruct((1024, 128), F32),
        in_specs=[whole] * 6,
        out_specs=whole,
        scratch_shapes=scratch,
        compiler_params=pltpu.CompilerParams(
            collective_id=0, has_side_effects=True, vmem_limit_bytes=48 * 2**20
        ),
        name="propagate",
    )(x, propagator, lengths, centrifugal, channel_pairs.T, strengths.reshape(1, 32))
    return out.reshape(8, 2, 16, 2, 2, 128).transpose(0, 1, 2, 4, 3, 5).reshape(shape)


def solution(mesh):
    in_specs = (P("pencil", None, None, "slab", None), P(), P("slab", "pencil"), P(), P(), P())
    out_specs = P("pencil", None, None, "slab", None)
    return jax.shard_map(
        on_device, mesh=mesh, in_specs=in_specs, out_specs=out_specs, check_vma=False
    )
```

```python
import jax
import jax.numpy as jnp
from jax import lax
from jax.experimental import pallas as pl
from jax.experimental.pallas import tpu as pltpu
from jax.sharding import PartitionSpec as P


MESH = pl.DeviceIdType.MESH
F32 = jnp.float32
BF16 = jnp.bfloat16
STEP = 0.1
GRID = 0.5
CHARGE = 3.0
BAND = 0.3
NP = 32
NS = 16
L2 = 8
L3 = 2
C = 16
N = 256
CHUNKS = 4


def iota(shape, dim):
    return lax.broadcasted_iota(jnp.int32, shape, dim)


def split2(x):
    high = x.astype(BF16)
    return high, (x - high.astype(F32)).astype(BF16)


def split3(x):
    high = x.astype(BF16)
    rest = x - high.astype(F32)
    middle = rest.astype(BF16)
    return high, middle, (rest - middle.astype(F32)).astype(BF16)


def product(a, b, contract=((1,), (0,))):
    def one(x, y):
        return lax.dot_general(x, y, (contract, ((), ())), preferred_element_type=F32)

    return one(a[0], b[0]) + (one(a[0], b[1]) + one(a[1], b[0]))


def column(row, count):
    shape = (count, row.shape[1])
    return jnp.sum(jnp.where(iota(shape, 0) == iota(shape, 1), row, jnp.zeros_like(row)), axis=1, keepdims=True)


def radial(position, weight):
    radius = GRID * (position.astype(F32) + 1.0)
    return -CHARGE / radius + weight / (radius * radius)


def flip_blocks(x):
    row, group = iota((1, 8, 128), 1), iota((1, 8, 128), 2) // 16
    for bit in (4, 2, 1):
        lanes = 16 * bit
        has_row, has_group = (row // bit) % 2, (group // bit) % 2
        down = pltpu.roll(pltpu.roll(x, bit, 1), 128 - lanes, 2)
        if bit == 4:
            up = down
        else:
            up = pltpu.roll(pltpu.roll(x, 8 - bit, 1), lanes, 2)
        x = jnp.where(has_row == has_group, x, jnp.where(has_row == 1, down, up))
    return x


def band(x):
    low = (iota((1, 1, 128), 2) // 32) % 2 == 0
    swapped = jnp.where(low, pltpu.roll(x, 96, 2), pltpu.roll(x, 32, 2))
    zero = jnp.zeros((1,) + x.shape[1:], F32)

    def before(a):
        return jnp.concatenate([zero, a[:-1]], axis=0)

    def after(a):
        return jnp.concatenate([a[1:], zero], axis=0)

    inner = swapped + jnp.where(low, before(swapped), after(swapped))
    return (BAND / 24.0) * (before(x) + after(x) - 16.0 * inner + 30.0 * x)


def body(
    x_hbm,
    prop_hbm,
    len_hbm,
    cent_hbm,
    pair_hbm,
    str_hbm,
    o_ref,
    x_ref,
    prop_ref,
    len_ref,
    cent_ref,
    pair_ref,
    str_ref,
    cos_a,
    sin_a,
    wl_a,
    lv_a,
    kron_hi,
    kron_lo,
    mix_hi,
    mix_lo,
    w1_hi,
    w1_lo,
    q2_hi,
    q2_lo,
    wf_hi,
    wf_lo,
    cos_d,
    sin_d,
    u_hi,
    u_lo,
    len_col,
    len_in,
    len_out,
    ybuf,
    bbuf,
    sbuf,
    dbuf,
    ebuf,
    hbuf,
    gbuf,
    rbuf,
    in_sem,
    send_sem,
    recv_sem,
    len_send,
    len_recv,
):
    p = lax.axis_index("pencil")
    s = lax.axis_index("slab")
    barrier = pltpu.get_barrier_semaphore()

    def far(n, size):
        half = (n + 1) // 2
        return size // 2 + (1 - 2 * (n % 2)) * half

    def pencil_peer(n):
        return lax.rem(p + far(n, NP), NP)

    def slab_peer(n):
        return lax.rem(s + far(n, NS), NS)

    @pl.loop(0, NP - 1)
    def _(n):
        pl.semaphore_signal(barrier, inc=1, device_id=(s, pencil_peer(n)), device_id_type=MESH)

    @pl.loop(0, NS - 1)
    def _(n):
        pl.semaphore_signal(barrier, inc=1, device_id=(slab_peer(n), p), device_id_type=MESH)

    pairs = [
        (pair_hbm, pair_ref),
        (str_hbm, str_ref),
        (cent_hbm, cent_ref),
        (len_hbm, len_ref),
        (x_hbm, x_ref),
        (prop_hbm, prop_ref),
    ]
    inputs = [pltpu.make_async_copy(src, dst, in_sem.at[i]) for i, (src, dst) in enumerate(pairs)]
    for item in inputs:
        item.start()

    def copy(src, dst, k, device):
        return pltpu.make_async_remote_copy(
            src_ref=src,
            dst_ref=dst,
            send_sem=send_sem.at[k],
            recv_sem=recv_sem.at[k],
            device_id=device,
            device_id_type=MESH,
        )

    def pencil_exchange(src, dst, chunk, k):
        @pl.loop(0, NP - 1)
        def _(n):
            q = pencil_peer(n)
            copy(src.at[chunk, q], dst.at[chunk, p], k, (s, q)).start()

        dst[chunk, pl.ds(p, 1)] = src[chunk, pl.ds(p, 1)]

    def slab_exchange(src, dst, chunk, k):
        @pl.loop(0, NS - 1)
        def _(n):
            q = slab_peer(n)
            copy(src.at[chunk, q], dst.at[chunk, s], k, (q, p)).start()

        dst[chunk, pl.ds(s, 1)] = src[chunk, pl.ds(s, 1)]

    def arrived(buf, chunk, k, count):
        part = buf.at[chunk, pl.ds(0, count - 1)]
        copy(part, part, k, (s, p)).wait_recv()

    def left(buf, chunk, k, count):
        part = buf.at[chunk, pl.ds(0, count - 1)]
        copy(part, part, k, (s, p)).wait_send()

    inputs[0].wait()
    inputs[1].wait()
    strength = str_ref[...]
    first, second = pair_ref[0:1, :], pair_ref[1:2, :]

    def hot_rows(labels):
        return (iota((N, 32), 0) % C == labels).astype(F32)

    def hot_cols(labels):
        shape = (32, 32)
        col = jnp.sum(jnp.where(iota(shape, 0) == iota(shape, 1), labels, 0), axis=1, keepdims=True)
        return (iota((32, N), 1) % C == col).astype(F32)

    rows_1, rows_2, cols_1, cols_2 = hot_rows(first), hot_rows(second), hot_cols(first), hot_cols(second)
    tiled = jnp.zeros((N, N), F32)
    for part in split3(strength):
        scale = part.astype(F32)
        tiled = tiled + jnp.dot((rows_1 * scale).astype(BF16), cols_2.astype(BF16), preferred_element_type=F32)
        tiled = tiled + jnp.dot((rows_2 * scale).astype(BF16), cols_1.astype(BF16), preferred_element_type=F32)
    row, col = iota((N, N), 0), iota((N, N), 1)
    kron_hi[...], kron_lo[...] = split2(jnp.where(row // C == col // C, tiled, 0.0))
    row, col = iota((128, 128), 0), iota((128, 128), 1)
    same = (row // C) % 4 == (col // C) % 4
    sign = (row // 64 - col // 64).astype(F32)
    mix_hi[...], mix_lo[...] = split2(jnp.where(same, tiled[:128, :128] * sign, 0.0))

    inputs[2].wait()
    inputs[3].wait()
    half = 0.5 * STEP
    cent = cent_ref[...]
    cent_col = [column(cent[e : e + 1], C) for e in range(3)]
    angle_1 = half * radial(iota((C, N), 1), cent_col[0])
    cos_1, sin_1 = jnp.cos(angle_1), jnp.sin(angle_1)
    lane = iota((C, 16), 1)
    angle_23 = half * (radial(L2 * p + lane % L2, cent_col[1]) + radial(L3 * s + lane // L2, cent_col[2]))
    cos_23, sin_23 = jnp.cos(angle_23), jnp.sin(angle_23)
    for m in range(16):
        c23, s23 = cos_23[:, m : m + 1], sin_23[:, m : m + 1]
        cos_a[m * C : (m + 1) * C] = cos_1 * c23 - sin_1 * s23
        sin_a[m * C : (m + 1) * C] = sin_1 * c23 + cos_1 * s23

    lens = len_ref[...].astype(F32)
    lane = iota((8, 128), 1)
    len_tile = jnp.zeros((8, 128), F32)
    len_rows = []
    for i3 in range(L3):
        col = column(lens[i3 : i3 + 1], L2)
        len_rows.append(col)
        len_tile = len_tile + jnp.where(lane == L3 * s + i3, col, jnp.zeros_like(col))
    len_out[0] = len_tile
    len_a = jnp.concatenate(len_rows, axis=0)

    row, col = iota((16, N), 0), iota((16, N), 1)
    farthest = jnp.maximum(jnp.maximum(L2 * p + row % L2, L3 * s + row // L2), col).astype(F32)
    live = (col.astype(F32) < len_a).astype(F32)
    lv_a[...] = live
    wl_a[...] = live * (half / (1.0 + 0.02 * farthest))

    inputs[4].wait()
    kron = (kron_hi[...], kron_lo[...])

    def potential(re, im):
        cosine, sine = cos_a[...], sin_a[...]
        turned_re = re * cosine + im * sine
        turned_im = im * cosine - re * sine
        mixed_re = product(kron, split2(turned_im))
        mixed_im = product(kron, split2(turned_re))

        def rows(a):
            return jnp.concatenate([jnp.broadcast_to(a[m : m + 1], (C, N)) for m in range(16)], axis=0)

        weight, alive = rows(wl_a[...]), rows(lv_a[...])
        return turned_re * alive + weight * mixed_re, turned_im * alive - weight * mixed_im

    def load(part):
        blocks = []
        for i3 in range(L3):
            for i2 in range(L2):
                base = (i2 * 2 + part) * 64 + i3
                blocks.append(
                    jnp.concatenate([x_ref[pl.ds(base + 2 * l, C, stride=4), :] for l in range(2)], axis=1)
                )
        return jnp.concatenate(blocks, axis=0)

    v_re, v_im = potential(load(0), load(1))
    u_hi[...], u_lo[...] = split2(jnp.concatenate([v_re, v_im], axis=1))
    u = (u_hi[...], u_lo[...])

    inputs[5].wait()
    sub = iota((1, 8, 2 * N), 1)

    def interleaved(re, im):
        top = jnp.concatenate([re, -im], axis=1).reshape(NP, 8, 2 * N)
        low = jnp.concatenate([im, re], axis=1).reshape(NP, 8, 2 * N)
        early = jnp.where(sub < 4, top, pltpu.roll(low, 4, 1))
        late = jnp.where(sub < 4, pltpu.roll(top, 4, 1), low)
        return [split2(v.reshape(N, 2 * N)) for v in (early, late)]

    for part, (high, low) in enumerate(interleaved(prop_ref[0], prop_ref[1])):
        w1_hi[part], w1_lo[part] = high, low

    outer = (iota((1, 8, 128), 1) // 2) % 2 == 0

    def first_line(half_of):
        y = product((w1_hi[half_of], w1_lo[half_of]), u, ((1,), (1,)))
        y = [y[:, i * 128 : (i + 1) * 128].reshape(NP, 8, 128) for i in range(L3)]
        ybuf[2 * half_of] = jnp.where(outer, y[0], pltpu.roll(y[1], 2, 1))
        ybuf[2 * half_of + 1] = jnp.where(outer, pltpu.roll(y[0], 6, 1), y[1])

    first_line(0)

    root = s == p // 2

    def len_copy(src, dst, k, device):
        return pltpu.make_async_remote_copy(
            src_ref=src,
            dst_ref=dst,
            send_sem=len_send.at[k],
            recv_sem=len_recv.at[k],
            device_id=device,
            device_id_type=MESH,
        )

    pl.semaphore_wait(barrier, NP + NS - 2)

    @pl.when(jnp.logical_not(root))
    def _():
        len_copy(len_out.at[0], len_col.at[s], 0, (p // 2, p)).start()

    pencil_exchange(ybuf, bbuf, 0, 0)
    first_line(1)

    @pl.when(root)
    def _():
        len_col[pl.ds(s, 1)] = len_out[pl.ds(0, 1)]
        part = len_col.at[pl.ds(0, NS - 1)]
        len_copy(part, part, 0, (s, p)).wait_recv()
        total = jnp.sum(len_col[...], axis=0)
        len_out[1] = total
        len_in[pl.ds(lax.rem(p, 2), 1)] = total[None]

        @pl.loop(0, NP - 1)
        def _(n):
            len_copy(len_out.at[1], len_in.at[lax.rem(p, 2)], 1, (s, pencil_peer(n))).start()

    for chunk in range(1, CHUNKS):
        pencil_exchange(ybuf, bbuf, chunk, chunk)

    re, im = prop_ref[0], prop_ref[1]
    q2_hi[...], q2_lo[...] = split2(jnp.concatenate([re, im], axis=0))
    for part, (high, low) in enumerate(interleaved(re.T, -im.T)):
        wf_hi[part], wf_lo[part] = high, low

    lane = iota((C, 128), 1)
    cent_row = [
        jnp.sum(jnp.where(iota((C, 128), 0) == lane % C, col, 0.0), axis=0, keepdims=True) for col in cent_col
    ]
    lane = iota((1, 128), 1)
    second_pos = 16 * s + iota((16, 128), 0)
    third_pos = L3 * iota((NS, 128), 0) + (lane // 32) % 2

    def first_pos(chunk):
        return 8 * p + 2 * chunk + (lane // C) % 2

    angle_2 = STEP * radial(second_pos, cent_row[1])
    angle_3 = STEP * radial(third_pos, cent_row[2])
    cos_3, sin_3 = jnp.cos(angle_3), jnp.sin(angle_3)
    turn = jnp.where(lane < 64, 1.0, -1.0)
    for chunk in range(CHUNKS):
        angle_12 = angle_2 + STEP * radial(first_pos(chunk), cent_row[0])
        cos_12, sin_12 = jnp.cos(angle_12), jnp.sin(angle_12)
        for i in range(NS):
            c3, s3 = cos_3[i : i + 1], sin_3[i : i + 1]
            cos_d[chunk, i] = cos_12 * c3 - sin_12 * s3
            sin_d[chunk, i] = turn * (sin_12 * c3 + cos_12 * s3)

    q2 = (q2_hi[...], q2_lo[...])

    def second_line(z):
        both = product(q2, split2(z))
        return both[:N] - turn * pltpu.roll(both[N:], 64, 1)

    def third_line(psi):
        g1 = band(psi)
        g2 = band(g1)
        return psi + turn * pltpu.roll(g1, 64, 2) - 0.5 * g2

    def third_potential(psi, chunk):
        turned = psi * cos_d[chunk] + sin_d[chunk] * pltpu.roll(psi, 64, 2)
        mixed = product(split2(turned.reshape(N, 128)), (mix_hi[...], mix_lo[...])).reshape(NS, 16, 128)
        position = first_pos(chunk)
        both = jnp.maximum(second_pos, position)
        lengths = jnp.concatenate([len_in[0], len_in[1]], axis=0)
        out = []
        for i in range(NS):
            weight = STEP / (1.0 + 0.02 * jnp.maximum(both, third_pos[i : i + 1]).astype(F32))
            end = jnp.where((lane // 32) % 2 == 0, lengths[:, L3 * i : L3 * i + 1], lengths[:, L3 * i + 1 : L3 * i + 2])
            out.append(jnp.where(position.astype(F32) < end, turned[i] + weight * mixed[i], 0.0))
        return jnp.stack(out, axis=0)

    def step_1(chunk):
        arrived(bbuf, chunk, chunk, NP)
        z = second_line(flip_blocks(bbuf[chunk]).reshape(N, 128))
        sbuf[chunk] = z.reshape(NS, 16, 128)
        slab_exchange(sbuf, dbuf, chunk, CHUNKS + chunk)

    def step_2(chunk):
        arrived(dbuf, chunk, CHUNKS + chunk, NS)
        psi = third_line(dbuf[chunk])
        ebuf[chunk] = third_line(third_potential(psi, chunk))
        slab_exchange(ebuf, hbuf, chunk, 2 * CHUNKS + chunk)

    def step_3(chunk):
        arrived(hbuf, chunk, 2 * CHUNKS + chunk, NS)
        z = second_line(hbuf[chunk].reshape(N, 128))
        gbuf[chunk] = flip_blocks(z.reshape(NP, 8, 128))
        pencil_exchange(gbuf, rbuf, chunk, 3 * CHUNKS + chunk)

    for chunk in range(CHUNKS):
        step_1(chunk)
        if chunk == 0:

            @pl.when(root)
            def _():
                len_copy(len_in.at[0], len_in.at[0], 1, (s, p)).wait_recv()

            @pl.when(jnp.logical_not(root))
            def _():
                len_copy(len_in, len_in, 1, (s, p)).wait_recv()

        else:
            step_3(chunk - 1)
        step_2(chunk)
    step_3(CHUNKS - 1)

    out = jnp.zeros((N, 2 * N), F32)
    for half_of in range(2):
        chunk = 2 * half_of
        arrived(rbuf, chunk, 3 * CHUNKS + chunk, NP)
        arrived(rbuf, chunk + 1, 3 * CHUNKS + chunk + 1, NP)
        t0, t1 = rbuf[chunk], rbuf[chunk + 1]
        r = [jnp.where(outer, t0, pltpu.roll(t1, 2, 1)), jnp.where(outer, pltpu.roll(t0, 6, 1), t1)]
        r = jnp.concatenate([a.reshape(N, 128) for a in r], axis=1)
        out = out + product(split2(r.T), (wf_hi[half_of], wf_lo[half_of]))

    out = potential(out[:, :N], out[:, N:])
    for part in range(2):
        for i3 in range(L3):
            for i2 in range(L2):
                base = (i2 * 2 + part) * 64 + i3
                start = (i3 * L2 + i2) * C
                for l in range(2):
                    o_ref[pl.ds(base + 2 * l, C, stride=4), :] = out[part][start : start + C, l * 128 : (l + 1) * 128]

    for chunk in range(CHUNKS):
        left(ybuf, chunk, chunk, NP)
        left(sbuf, chunk, CHUNKS + chunk, NS)
        left(ebuf, chunk, 2 * CHUNKS + chunk, NS)
        left(gbuf, chunk, 3 * CHUNKS + chunk, NP)

    @pl.when(root)
    def _():
        @pl.loop(0, NP - 1)
        def _(n):
            len_copy(len_out.at[1], len_in.at[0], 1, (s, p)).wait_send()

    @pl.when(jnp.logical_not(root))
    def _():
        len_copy(len_out.at[0], len_col.at[0], 0, (s, p)).wait_send()


def on_device(wavefunction, propagator, lengths, centrifugal, channel_pairs, strengths):
    shape = wavefunction.shape
    x = wavefunction.reshape(8, 2, 16, 2, 2, 128).transpose(0, 1, 2, 4, 3, 5).reshape(1024, 128)
    operands = (x, propagator, lengths, centrifugal, channel_pairs.T, strengths.reshape(1, 32))

    def vmem(*dims, dtype=F32):
        return pltpu.VMEM(dims, dtype)

    scratch = [pltpu.VMEM(a.shape, a.dtype) for a in operands]
    scratch += [
        vmem(N, N),
        vmem(N, N),
        vmem(16, N),
        vmem(16, N),
        vmem(N, N, dtype=BF16),
        vmem(N, N, dtype=BF16),
        vmem(128, 128, dtype=BF16),
        vmem(128, 128, dtype=BF16),
        vmem(2, N, 2 * N, dtype=BF16),
        vmem(2, N, 2 * N, dtype=BF16),
        vmem(2 * N, N, dtype=BF16),
        vmem(2 * N, N, dtype=BF16),
        vmem(2, N, 2 * N, dtype=BF16),
        vmem(2, N, 2 * N, dtype=BF16),
        vmem(CHUNKS, NS, 16, 128),
        vmem(CHUNKS, NS, 16, 128),
        vmem(N, 2 * N, dtype=BF16),
        vmem(N, 2 * N, dtype=BF16),
        vmem(NS, 8, 128),
        vmem(2, 8, 128),
        vmem(2, 8, 128),
        vmem(CHUNKS, NP, 8, 128),
        vmem(CHUNKS, NP, 8, 128),
        vmem(CHUNKS, NS, 16, 128),
        vmem(CHUNKS, NS, 16, 128),
        vmem(CHUNKS, NS, 16, 128),
        vmem(CHUNKS, NS, 16, 128),
        vmem(CHUNKS, NP, 8, 128),
        vmem(CHUNKS, NP, 8, 128),
        pltpu.SemaphoreType.DMA((6,)),
        pltpu.SemaphoreType.DMA((4 * CHUNKS,)),
        pltpu.SemaphoreType.DMA((4 * CHUNKS,)),
        pltpu.SemaphoreType.DMA((2,)),
        pltpu.SemaphoreType.DMA((2,)),
    ]
    out = pl.pallas_call(
        body,
        out_shape=jax.ShapeDtypeStruct((1024, 128), F32),
        in_specs=[pl.BlockSpec(memory_space=pltpu.HBM)] * 6,
        out_specs=pl.BlockSpec(memory_space=pltpu.VMEM),
        scratch_shapes=scratch,
        compiler_params=pltpu.CompilerParams(
            collective_id=0, has_side_effects=True, vmem_limit_bytes=60 * 2**20
        ),
        name="propagate",
    )(*operands)
    return out.reshape(8, 2, 16, 2, 2, 128).transpose(0, 1, 2, 4, 3, 5).reshape(shape)


def solution(mesh):
    in_specs = (P("pencil", None, None, "slab", None), P(), P("slab", "pencil"), P(), P(), P())
    out_specs = P("pencil", None, None, "slab", None)
    return jax.shard_map(
        on_device, mesh=mesh, in_specs=in_specs, out_specs=out_specs, check_vma=False
    )
```

```python
import jax
import jax.numpy as jnp
from jax import lax
from jax.experimental import pallas as pl
from jax.experimental.pallas import tpu as pltpu
from jax.sharding import PartitionSpec as P


MESH = pl.DeviceIdType.MESH
F32 = jnp.float32
BF16 = jnp.bfloat16
STEP = 0.1
GRID = 0.5
CHARGE = 3.0
BAND = 0.3
NP = 32
NS = 16
L2 = 8
L3 = 2
C = 16
N = 256
CHUNKS = 2


def iota(shape, dim):
    return lax.broadcasted_iota(jnp.int32, shape, dim)


def split2(x):
    high = x.astype(BF16)
    return high, (x - high.astype(F32)).astype(BF16)


def split3(x):
    high = x.astype(BF16)
    rest = x - high.astype(F32)
    middle = rest.astype(BF16)
    return high, middle, (rest - middle.astype(F32)).astype(BF16)


def product(a, b, contract=((1,), (0,))):
    def one(x, y):
        return lax.dot_general(x, y, (contract, ((), ())), preferred_element_type=F32)

    return one(a[0], b[0]) + (one(a[0], b[1]) + one(a[1], b[0]))


def column(row, count):
    shape = (count, row.shape[1])
    return jnp.sum(jnp.where(iota(shape, 0) == iota(shape, 1), row, jnp.zeros_like(row)), axis=1, keepdims=True)


def radial(position, weight):
    radius = GRID * (position.astype(F32) + 1.0)
    return -CHARGE / radius + weight / (radius * radius)


def flip_blocks(x):
    row, group = iota((1, 8, 128), 1), iota((1, 8, 128), 2) // 16
    for bit in (4, 2, 1):
        lanes = 16 * bit
        has_row, has_group = (row // bit) % 2, (group // bit) % 2
        down = pltpu.roll(pltpu.roll(x, bit, 1), 128 - lanes, 2)
        if bit == 4:
            up = down
        else:
            up = pltpu.roll(pltpu.roll(x, 8 - bit, 1), lanes, 2)
        x = jnp.where(has_row == has_group, x, jnp.where(has_row == 1, down, up))
    return x


def band(x):
    low = (iota((1, 1, 128), 2) // 32) % 2 == 0
    swapped = jnp.where(low, pltpu.roll(x, 96, 2), pltpu.roll(x, 32, 2))
    zero = jnp.zeros((1,) + x.shape[1:], F32)

    def before(a):
        return jnp.concatenate([zero, a[:-1]], axis=0)

    def after(a):
        return jnp.concatenate([a[1:], zero], axis=0)

    inner = swapped + jnp.where(low, before(swapped), after(swapped))
    return (BAND / 24.0) * (before(x) + after(x) - 16.0 * inner + 30.0 * x)


def body(
    x_hbm,
    prop_hbm,
    len_hbm,
    cent_hbm,
    pair_hbm,
    str_hbm,
    o_ref,
    x_ref,
    prop_ref,
    len_ref,
    cent_ref,
    pair_ref,
    str_ref,
    cos_a,
    sin_a,
    wl_a,
    lv_a,
    kron_hi,
    kron_lo,
    mix_hi,
    mix_lo,
    w1_hi,
    w1_lo,
    q2_hi,
    q2_lo,
    wf_hi,
    wf_lo,
    cos_d,
    sin_d,
    u_hi,
    u_lo,
    len_col,
    len_in,
    len_out,
    ybuf,
    bbuf,
    sbuf,
    dbuf,
    ebuf,
    hbuf,
    gbuf,
    rbuf,
    cos_e,
    sin_e,
    wt_e,
    len_row,
    edge_in,
    edge_out,
    e_ybuf,
    e_cbuf,
    e_kbuf,
    e_bbuf,
    e_gbuf,
    e_hbuf,
    e_fbuf,
    e_rbuf,
    in_sem,
    send_sem,
    recv_sem,
    len_send,
    len_recv,
):
    p = lax.axis_index("pencil")
    s = lax.axis_index("slab")
    pairs = [
        (pair_hbm, pair_ref),
        (str_hbm, str_ref),
        (cent_hbm, cent_ref),
        (len_hbm, len_ref),
        (x_hbm, x_ref),
        (prop_hbm, prop_ref),
    ]
    inputs = [pltpu.make_async_copy(src, dst, in_sem.at[i]) for i, (src, dst) in enumerate(pairs)]
    for item in inputs:
        item.start()

    barrier = pltpu.get_barrier_semaphore()

    def far(n, size):
        half = (n + 1) // 2
        return size // 2 + (1 - 2 * (n % 2)) * half

    def pencil_peer(n):
        return lax.rem(p + far(n, NP), NP)

    def slab_peer(n):
        return lax.rem(s + far(n, NS), NS)

    @pl.loop(0, NP - 1)
    def _(n):
        pl.semaphore_signal(barrier, inc=1, device_id=(s, pencil_peer(n)), device_id_type=MESH)

    @pl.loop(0, NS - 1)
    def _(n):
        pl.semaphore_signal(barrier, inc=1, device_id=(slab_peer(n), p), device_id_type=MESH)

    def copy(src, dst, k, device):
        return pltpu.make_async_remote_copy(
            src_ref=src,
            dst_ref=dst,
            send_sem=send_sem.at[k],
            recv_sem=recv_sem.at[k],
            device_id=device,
            device_id_type=MESH,
        )

    def pencil_exchange(src, dst, chunk, k):
        @pl.loop(0, NP - 1)
        def _(n):
            q = pencil_peer(n)
            copy(src.at[chunk, q], dst.at[chunk, p], k, (s, q)).start()

        dst[chunk, pl.ds(p, 1)] = src[chunk, pl.ds(p, 1)]

    def slab_exchange(src, dst, chunk, k):
        @pl.loop(0, NS - 1)
        def _(n):
            q = slab_peer(n)
            copy(src.at[chunk, q], dst.at[chunk, s], k, (q, p)).start()

        dst[chunk, pl.ds(s, 1)] = src[chunk, pl.ds(s, 1)]

    def arrived(buf, chunk, k, count):
        part = buf.at[chunk, pl.ds(0, count - 1)]
        copy(part, part, k, (s, p)).wait_recv()

    def left(buf, chunk, k, count):
        part = buf.at[chunk, pl.ds(0, count - 1)]
        copy(part, part, k, (s, p)).wait_send()

    inputs[0].wait()
    inputs[1].wait()
    strength = str_ref[...]
    first, second = pair_ref[0:1, :], pair_ref[1:2, :]

    def hot_rows(labels):
        return (iota((N, 32), 0) % C == labels).astype(F32)

    def hot_cols(labels):
        shape = (32, 32)
        col = jnp.sum(jnp.where(iota(shape, 0) == iota(shape, 1), labels, 0), axis=1, keepdims=True)
        return (iota((32, N), 1) % C == col).astype(F32)

    rows_1, rows_2, cols_1, cols_2 = hot_rows(first), hot_rows(second), hot_cols(first), hot_cols(second)
    tiled = jnp.zeros((N, N), F32)
    for part in split3(strength):
        scale = part.astype(F32)
        tiled = tiled + jnp.dot((rows_1 * scale).astype(BF16), cols_2.astype(BF16), preferred_element_type=F32)
        tiled = tiled + jnp.dot((rows_2 * scale).astype(BF16), cols_1.astype(BF16), preferred_element_type=F32)
    row, col = iota((N, N), 0), iota((N, N), 1)
    kron_hi[...], kron_lo[...] = split2(jnp.where(row // C == col // C, tiled, 0.0))
    row, col = iota((128, 128), 0), iota((128, 128), 1)
    same = (row // C) % 4 == (col // C) % 4
    sign = (row // 64 - col // 64).astype(F32)
    mix_hi[...], mix_lo[...] = split2(jnp.where(same, tiled[:128, :128] * sign, 0.0))

    inputs[2].wait()
    inputs[3].wait()
    half = 0.5 * STEP
    cent = cent_ref[...]
    cent_col = [column(cent[e : e + 1], C) for e in range(3)]
    angle_1 = half * radial(iota((C, N), 1), cent_col[0])
    cos_1, sin_1 = jnp.cos(angle_1), jnp.sin(angle_1)
    lane = iota((C, 16), 1)
    angle_23 = half * (radial(L2 * p + lane % L2, cent_col[1]) + radial(L3 * s + lane // L2, cent_col[2]))
    cos_23, sin_23 = jnp.cos(angle_23), jnp.sin(angle_23)
    for m in range(16):
        c23, s23 = cos_23[:, m : m + 1], sin_23[:, m : m + 1]
        cos_a[m * C : (m + 1) * C] = cos_1 * c23 - sin_1 * s23
        sin_a[m * C : (m + 1) * C] = sin_1 * c23 + cos_1 * s23

    lens = len_ref[...].astype(F32)
    lane = iota((8, 128), 1)
    len_tile = jnp.zeros((8, 128), F32)
    len_rows = []
    for i3 in range(L3):
        col = column(lens[i3 : i3 + 1], L2)
        len_rows.append(col)
        edge_out[i3] = jnp.where(lane == p, col, jnp.zeros_like(col))
        len_tile = len_tile + jnp.where(lane == L3 * s + i3, col, jnp.zeros_like(col))
    len_out[0] = len_tile
    len_a = jnp.concatenate(len_rows, axis=0)

    row, col = iota((16, N), 0), iota((16, N), 1)
    farthest = jnp.maximum(jnp.maximum(L2 * p + row % L2, L3 * s + row // L2), col).astype(F32)
    live = (col.astype(F32) < len_a).astype(F32)
    lv_a[...] = live
    wl_a[...] = live * (half / (1.0 + 0.02 * farthest))

    inputs[4].wait()
    kron = (kron_hi[...], kron_lo[...])

    def potential(re, im):
        cosine, sine = cos_a[...], sin_a[...]
        turned_re = re * cosine + im * sine
        turned_im = im * cosine - re * sine
        mixed_re = product(kron, split2(turned_im))
        mixed_im = product(kron, split2(turned_re))

        def rows(a):
            return jnp.concatenate([jnp.broadcast_to(a[m : m + 1], (C, N)) for m in range(16)], axis=0)

        weight, alive = rows(wl_a[...]), rows(lv_a[...])
        return turned_re * alive + weight * mixed_re, turned_im * alive - weight * mixed_im

    def load(part):
        blocks = []
        for i3 in range(L3):
            for i2 in range(L2):
                base = (i2 * 2 + part) * 64 + i3
                blocks.append(
                    jnp.concatenate([x_ref[pl.ds(base + 2 * l, C, stride=4), :] for l in range(2)], axis=1)
                )
        return jnp.concatenate(blocks, axis=0)

    v_re, v_im = potential(load(0), load(1))
    u_hi[...], u_lo[...] = split2(jnp.concatenate([v_re, v_im], axis=1))
    u = (u_hi[...], u_lo[...])

    inputs[5].wait()
    sub = iota((1, 8, 2 * N), 1)

    def interleaved(re, im):
        top = jnp.concatenate([re, -im], axis=1).reshape(NP, 8, 2 * N)
        low = jnp.concatenate([im, re], axis=1).reshape(NP, 8, 2 * N)
        early = jnp.where(sub < 4, top, pltpu.roll(low, 4, 1))
        late = jnp.where(sub < 4, pltpu.roll(top, 4, 1), low)
        return [split2(v.reshape(N, 2 * N)) for v in (early, late)]

    for part, (high, low) in enumerate(interleaved(prop_ref[0], prop_ref[1])):
        w1_hi[part], w1_lo[part] = high, low

    outer = (iota((1, 8, 128), 1) // 2) % 2 == 0

    def first_line(half_of):
        y = product((w1_hi[half_of], w1_lo[half_of]), u, ((1,), (1,)))
        return [y[:, i * 128 : (i + 1) * 128] for i in range(L3)]

    y = [a.reshape(NP, 8, 128) for a in first_line(0)]
    ybuf[0] = jnp.where(outer, y[0], pltpu.roll(y[1], 2, 1))
    ybuf[1] = jnp.where(outer, pltpu.roll(y[0], 6, 1), y[1])

    root = s == p // 2

    def len_copy(src, dst, k, device):
        return pltpu.make_async_remote_copy(
            src_ref=src,
            dst_ref=dst,
            send_sem=len_send.at[k],
            recv_sem=len_recv.at[k],
            device_id=device,
            device_id_type=MESH,
        )

    pl.semaphore_wait(barrier, NP + NS - 2)

    @pl.when(jnp.logical_not(root))
    def _():
        len_copy(len_out.at[0], len_col.at[s], 0, (p // 2, p)).start()

    for i3 in range(L3):

        @pl.when(p != L3 * s + i3)
        def _():
            len_copy(edge_out.at[i3], len_row.at[p], 2 + i3, (s, L3 * s + i3)).start()

    pencil_exchange(ybuf, bbuf, 0, 0)

    y = first_line(1)
    for chunk in range(CHUNKS):
        for i3 in range(L3):
            e_ybuf[chunk, :, i3] = y[i3].reshape(NS, CHUNKS, 8, 128)[:, chunk]
        slab_exchange(e_ybuf, e_cbuf, chunk, 4 * CHUNKS + chunk)

    @pl.when(root)
    def _():
        len_col[pl.ds(s, 1)] = len_out[pl.ds(0, 1)]
        part = len_col.at[pl.ds(0, NS - 1)]
        len_copy(part, part, 0, (s, p)).wait_recv()
        total = jnp.sum(len_col[...], axis=0)
        len_out[1] = total
        len_in[pl.ds(lax.rem(p, 2), 1)] = total[None]

        @pl.loop(0, NP - 1)
        def _(n):
            len_copy(len_out.at[1], len_in.at[lax.rem(p, 2)], 1, (s, pencil_peer(n))).start()

    def edge_third(x):
        zero = jnp.zeros((2,) + x.shape[1:], F32)

        def band_first(a):
            b = jnp.concatenate([zero, a, zero], axis=0)
            return (BAND / 24.0) * (b[:32] + b[4:36] - 16.0 * (b[1:33] + b[3:35]) + 30.0 * a)

        g1 = band_first(x)
        g2 = band_first(g1)
        sign = jnp.where(iota((1, 8, 128), 1) < 4, 1.0, -1.0)
        return x + sign * pltpu.roll(g1, 4, 1) - 0.5 * g2

    def edge_1(chunk):
        arrived(e_cbuf, chunk, 4 * CHUNKS + chunk, NS)
        e_kbuf[chunk] = edge_third(e_cbuf[chunk].reshape(NP, 8, 128))
        pencil_exchange(e_kbuf, e_bbuf, chunk, 5 * CHUNKS + chunk)

    re, im = prop_ref[0], prop_ref[1]
    q2_hi[...], q2_lo[...] = split2(jnp.concatenate([re, im], axis=0))

    edge_1(0)
    pencil_exchange(ybuf, bbuf, 1, 1)
    edge_1(1)

    @pl.when(root)
    def _():
        len_row[pl.ds(p, 1)] = edge_out[pl.ds(lax.rem(p, 2), 1)]
        part = len_row.at[pl.ds(0, NP - 1)]
        len_copy(part, part, 2 + lax.rem(p, 2), (s, p)).wait_recv()
        total = jnp.sum(len_row[...], axis=0)
        edge_out[2] = total
        edge_in[0] = total

        @pl.loop(0, NS - 1)
        def _(n):
            len_copy(edge_out.at[2], edge_in.at[0], 4, (slab_peer(n), p)).start()

    for part, (high, low) in enumerate(interleaved(re.T, -im.T)):
        wf_hi[part], wf_lo[part] = high, low

    lane = iota((C, 128), 1)
    cent_row = [
        jnp.sum(jnp.where(iota((C, 128), 0) == lane % C, col, 0.0), axis=0, keepdims=True) for col in cent_col
    ]
    lane = iota((1, 128), 1)
    second_pos = 16 * s + iota((16, 128), 0)
    third_pos = L3 * iota((NS, 128), 0) + (lane // 32) % 2

    def first_pos(chunk):
        return 8 * p + 2 * chunk + (lane // C) % 2

    angle_2 = STEP * radial(second_pos, cent_row[1])
    angle_3 = STEP * radial(third_pos, cent_row[2])
    cos_3, sin_3 = jnp.cos(angle_3), jnp.sin(angle_3)
    turn = jnp.where(lane < 64, 1.0, -1.0)
    for chunk in range(CHUNKS):
        angle_12 = angle_2 + STEP * radial(first_pos(chunk), cent_row[0])
        cos_12, sin_12 = jnp.cos(angle_12), jnp.sin(angle_12)
        for i in range(NS):
            c3, s3 = cos_3[i : i + 1], sin_3[i : i + 1]
            cos_d[chunk, i] = cos_12 * c3 - sin_12 * s3
            sin_d[chunk, i] = turn * (sin_12 * c3 + cos_12 * s3)

    angle_2 = STEP * radial(iota((N, 128), 0), cent_row[1])
    cos_2, sin_2 = jnp.cos(angle_2), jnp.sin(angle_2)
    edge_rows = iota((N, 128), 0)

    def edge_first_pos(chunk):
        return 8 * (CHUNKS * s + chunk) + 4 + (lane // C) % 4

    for chunk in range(CHUNKS):
        position = edge_first_pos(chunk)
        angle_13 = STEP * (radial(position, cent_row[0]) + radial(jnp.full((1, 128), p, jnp.int32), cent_row[2]))
        cos_13, sin_13 = jnp.cos(angle_13), jnp.sin(angle_13)
        cos_e[chunk] = cos_2 * cos_13 - sin_2 * sin_13
        sin_e[chunk] = turn * (sin_2 * cos_13 + cos_2 * sin_13)
        farthest = jnp.maximum(jnp.maximum(edge_rows, position), p).astype(F32)
        wt_e[chunk] = STEP / (1.0 + 0.02 * farthest)

    q2 = (q2_hi[...], q2_lo[...])

    def second_line(z):
        both = product(q2, split2(z))
        return both[:N] - turn * pltpu.roll(both[N:], 64, 1)

    def third_line(psi):
        g1 = band(psi)
        g2 = band(g1)
        return psi + turn * pltpu.roll(g1, 64, 2) - 0.5 * g2

    def third_potential(psi, chunk):
        turned = psi * cos_d[chunk] + sin_d[chunk] * pltpu.roll(psi, 64, 2)
        mixed = product(split2(turned.reshape(N, 128)), (mix_hi[...], mix_lo[...])).reshape(NS, 16, 128)
        position = first_pos(chunk)
        both = jnp.maximum(second_pos, position)
        lengths = jnp.concatenate([len_in[0], len_in[1]], axis=0)
        out = []
        for i in range(NS):
            weight = STEP / (1.0 + 0.02 * jnp.maximum(both, third_pos[i : i + 1]).astype(F32))
            end = jnp.where((lane // 32) % 2 == 0, lengths[:, L3 * i : L3 * i + 1], lengths[:, L3 * i + 1 : L3 * i + 2])
            out.append(jnp.where(position.astype(F32) < end, turned[i] + weight * mixed[i], 0.0))
        return jnp.stack(out, axis=0)

    def step_1(chunk):
        arrived(bbuf, chunk, chunk, NP)
        z = second_line(flip_blocks(bbuf[chunk]).reshape(N, 128))
        sbuf[chunk] = z.reshape(NS, 16, 128)
        slab_exchange(sbuf, dbuf, chunk, CHUNKS + chunk)

    def step_2(chunk):
        arrived(dbuf, chunk, CHUNKS + chunk, NS)
        psi = third_line(dbuf[chunk])
        ebuf[chunk] = third_line(third_potential(psi, chunk))
        slab_exchange(ebuf, hbuf, chunk, 2 * CHUNKS + chunk)

    def step_3(chunk):
        arrived(hbuf, chunk, 2 * CHUNKS + chunk, NS)
        z = second_line(hbuf[chunk].reshape(N, 128))
        gbuf[chunk] = flip_blocks(z.reshape(NP, 8, 128))
        pencil_exchange(gbuf, rbuf, chunk, 3 * CHUNKS + chunk)

    def edge_potential(psi, chunk):
        turned = psi * cos_e[chunk] + sin_e[chunk] * pltpu.roll(psi, 64, 1)
        mixed = product(split2(turned), (mix_hi[...], mix_lo[...]))
        lengths = edge_in[0]
        end = jnp.concatenate([jnp.broadcast_to(lengths[:, i : i + 1], (8, 128)) for i in range(NP)], axis=0)
        return jnp.where(edge_first_pos(chunk).astype(F32) < end, turned + wt_e[chunk] * mixed, 0.0)

    def edge_2(chunk):
        arrived(e_bbuf, chunk, 5 * CHUNKS + chunk, NP)
        z = second_line(flip_blocks(e_bbuf[chunk]).reshape(N, 128))
        z = second_line(edge_potential(z, chunk))
        e_gbuf[chunk] = flip_blocks(z.reshape(NP, 8, 128))
        pencil_exchange(e_gbuf, e_hbuf, chunk, 6 * CHUNKS + chunk)

    def edge_3(chunk):
        arrived(e_hbuf, chunk, 6 * CHUNKS + chunk, NP)
        e_fbuf[chunk] = edge_third(e_hbuf[chunk]).reshape(NS, L3, 8, 128)
        slab_exchange(e_fbuf, e_rbuf, chunk, 7 * CHUNKS + chunk)

    step_1(0)

    @pl.when(root)
    def _():
        len_copy(len_in.at[0], len_in.at[0], 1, (s, p)).wait_recv()

    @pl.when(jnp.logical_not(root))
    def _():
        len_copy(len_in, len_in, 1, (s, p)).wait_recv()
        len_copy(edge_in, edge_in, 4, (s, p)).wait_recv()

    edge_2(0)
    step_2(0)
    step_1(1)
    step_3(0)
    edge_2(1)
    step_2(1)
    step_3(1)

    edge_3(0)
    edge_3(1)
    for chunk in range(CHUNKS):
        arrived(rbuf, chunk, 3 * CHUNKS + chunk, NP)
    t0, t1 = rbuf[0], rbuf[1]
    r = [jnp.where(outer, t0, pltpu.roll(t1, 2, 1)), jnp.where(outer, pltpu.roll(t0, 6, 1), t1)]
    r = jnp.concatenate([a.reshape(N, 128) for a in r], axis=1)
    out = product(split2(r.T), (wf_hi[0], wf_lo[0]))
    for chunk in range(CHUNKS):
        arrived(e_rbuf, chunk, 7 * CHUNKS + chunk, NS)
    r = [jnp.stack([e_rbuf[chunk, :, i3] for chunk in range(CHUNKS)], axis=1).reshape(N, 128) for i3 in range(L3)]
    out = out + product(split2(jnp.concatenate(r, axis=1).T), (wf_hi[1], wf_lo[1]))

    out = potential(out[:, :N], out[:, N:])
    for part in range(2):
        for i3 in range(L3):
            for i2 in range(L2):
                base = (i2 * 2 + part) * 64 + i3
                start = (i3 * L2 + i2) * C
                for l in range(2):
                    o_ref[pl.ds(base + 2 * l, C, stride=4), :] = out[part][start : start + C, l * 128 : (l + 1) * 128]

    for chunk in range(CHUNKS):
        left(ybuf, chunk, chunk, NP)
        left(sbuf, chunk, CHUNKS + chunk, NS)
        left(ebuf, chunk, 2 * CHUNKS + chunk, NS)
        left(gbuf, chunk, 3 * CHUNKS + chunk, NP)
        left(e_ybuf, chunk, 4 * CHUNKS + chunk, NS)
        left(e_kbuf, chunk, 5 * CHUNKS + chunk, NP)
        left(e_gbuf, chunk, 6 * CHUNKS + chunk, NP)
        left(e_fbuf, chunk, 7 * CHUNKS + chunk, NS)

    @pl.when(root)
    def _():
        @pl.loop(0, NP - 1)
        def _(n):
            len_copy(len_out.at[1], len_in.at[0], 1, (s, p)).wait_send()

        @pl.loop(0, NS - 1)
        def _(n):
            len_copy(edge_out.at[2], edge_in.at[0], 4, (s, p)).wait_send()

    @pl.when(jnp.logical_not(root))
    def _():
        len_copy(len_out.at[0], len_col.at[0], 0, (s, p)).wait_send()

    for i3 in range(L3):

        @pl.when(p != L3 * s + i3)
        def _():
            len_copy(edge_out.at[i3], len_row.at[0], 2 + i3, (s, p)).wait_send()


def on_device(wavefunction, propagator, lengths, centrifugal, channel_pairs, strengths):
    shape = wavefunction.shape
    x = wavefunction.reshape(8, 2, 16, 2, 2, 128).transpose(0, 1, 2, 4, 3, 5).reshape(1024, 128)
    operands = (x, propagator, lengths, centrifugal, channel_pairs.T, strengths.reshape(1, 32))

    def vmem(*dims, dtype=F32):
        return pltpu.VMEM(dims, dtype)

    scratch = [pltpu.VMEM(a.shape, a.dtype) for a in operands]
    scratch += [
        vmem(N, N),
        vmem(N, N),
        vmem(16, N),
        vmem(16, N),
        vmem(N, N, dtype=BF16),
        vmem(N, N, dtype=BF16),
        vmem(128, 128, dtype=BF16),
        vmem(128, 128, dtype=BF16),
        vmem(2, N, 2 * N, dtype=BF16),
        vmem(2, N, 2 * N, dtype=BF16),
        vmem(2 * N, N, dtype=BF16),
        vmem(2 * N, N, dtype=BF16),
        vmem(2, N, 2 * N, dtype=BF16),
        vmem(2, N, 2 * N, dtype=BF16),
        vmem(CHUNKS, NS, 16, 128),
        vmem(CHUNKS, NS, 16, 128),
        vmem(N, 2 * N, dtype=BF16),
        vmem(N, 2 * N, dtype=BF16),
        vmem(NS, 8, 128),
        vmem(2, 8, 128),
        vmem(2, 8, 128),
        vmem(CHUNKS, NP, 8, 128),
        vmem(CHUNKS, NP, 8, 128),
        vmem(CHUNKS, NS, 16, 128),
        vmem(CHUNKS, NS, 16, 128),
        vmem(CHUNKS, NS, 16, 128),
        vmem(CHUNKS, NS, 16, 128),
        vmem(CHUNKS, NP, 8, 128),
        vmem(CHUNKS, NP, 8, 128),
        vmem(CHUNKS, N, 128),
        vmem(CHUNKS, N, 128),
        vmem(CHUNKS, N, 128),
        vmem(NP, 8, 128),
        vmem(1, 8, 128),
        vmem(3, 8, 128),
        vmem(CHUNKS, NS, L3, 8, 128),
        vmem(CHUNKS, NS, L3, 8, 128),
        vmem(CHUNKS, NP, 8, 128),
        vmem(CHUNKS, NP, 8, 128),
        vmem(CHUNKS, NP, 8, 128),
        vmem(CHUNKS, NP, 8, 128),
        vmem(CHUNKS, NS, L3, 8, 128),
        vmem(CHUNKS, NS, L3, 8, 128),
        pltpu.SemaphoreType.DMA((6,)),
        pltpu.SemaphoreType.DMA((8 * CHUNKS,)),
        pltpu.SemaphoreType.DMA((8 * CHUNKS,)),
        pltpu.SemaphoreType.DMA((5,)),
        pltpu.SemaphoreType.DMA((5,)),
    ]
    out = pl.pallas_call(
        body,
        out_shape=jax.ShapeDtypeStruct((1024, 128), F32),
        in_specs=[pl.BlockSpec(memory_space=pltpu.HBM)] * 6,
        out_specs=pl.BlockSpec(memory_space=pltpu.VMEM),
        scratch_shapes=scratch,
        compiler_params=pltpu.CompilerParams(
            collective_id=0, has_side_effects=True, vmem_limit_bytes=53 * 2**20
        ),
        name="propagate",
    )(*operands)
    return out.reshape(8, 2, 16, 2, 2, 128).transpose(0, 1, 2, 4, 3, 5).reshape(shape)


def solution(mesh):
    in_specs = (P("pencil", None, None, "slab", None), P(), P("slab", "pencil"), P(), P(), P())
    out_specs = P("pencil", None, None, "slab", None)
    return jax.shard_map(
        on_device, mesh=mesh, in_specs=in_specs, out_specs=out_specs, check_vma=False
    )
```

```python
import jax
import jax.numpy as jnp
from jax import lax
from jax.experimental import pallas as pl
from jax.experimental.pallas import tpu as pltpu
from jax.sharding import PartitionSpec as P


MESH = pl.DeviceIdType.MESH
F32 = jnp.float32
BF16 = jnp.bfloat16
STEP = 0.1
GRID = 0.5
CHARGE = 3.0
BAND = 0.3
NP = 32
NS = 16
L2 = 8
L3 = 2
C = 16
N = 256
CHUNKS = 2


def iota(shape, dim):
    return lax.broadcasted_iota(jnp.int32, shape, dim)


def split2(x):
    high = x.astype(BF16)
    return high, (x - high.astype(F32)).astype(BF16)


def split3(x):
    high = x.astype(BF16)
    rest = x - high.astype(F32)
    middle = rest.astype(BF16)
    return high, middle, (rest - middle.astype(F32)).astype(BF16)


def product(a, b, contract=((1,), (0,))):
    def one(x, y):
        return lax.dot_general(x, y, (contract, ((), ())), preferred_element_type=F32)

    return one(a[0], b[0]) + (one(a[0], b[1]) + one(a[1], b[0]))


def column(row, count):
    shape = (count, row.shape[1])
    return jnp.sum(jnp.where(iota(shape, 0) == iota(shape, 1), row, jnp.zeros_like(row)), axis=1, keepdims=True)


def radial(position, weight):
    radius = GRID * (position.astype(F32) + 1.0)
    return -CHARGE / radius + weight / (radius * radius)


def flip_blocks(x):
    row, group = iota((1, 8, 128), 1), iota((1, 8, 128), 2) // 16
    for bit in (4, 2, 1):
        lanes = 16 * bit
        has_row, has_group = (row // bit) % 2, (group // bit) % 2
        down = pltpu.roll(pltpu.roll(x, bit, 1), 128 - lanes, 2)
        if bit == 4:
            up = down
        else:
            up = pltpu.roll(pltpu.roll(x, 8 - bit, 1), lanes, 2)
        x = jnp.where(has_row == has_group, x, jnp.where(has_row == 1, down, up))
    return x


def band(x):
    zero = jnp.zeros((2,) + x.shape[1:], F32)
    y = jnp.concatenate([zero, x, zero], axis=0)
    return (BAND / 24.0) * (y[:32] + y[4:36] - 16.0 * (y[1:33] + y[3:35]) + 30.0 * x)


def body(
    x_hbm,
    prop_hbm,
    len_hbm,
    cent_hbm,
    pair_hbm,
    str_hbm,
    o_ref,
    x_ref,
    prop_ref,
    len_ref,
    cent_ref,
    pair_ref,
    str_ref,
    cos_a,
    sin_a,
    wl_a,
    lv_a,
    kron_hi,
    kron_lo,
    mix_hi,
    mix_lo,
    w1_hi,
    w1_lo,
    q2_hi,
    q2_lo,
    wf_hi,
    wf_lo,
    cos_d,
    sin_d,
    u_hi,
    u_lo,
    len_col,
    len_in,
    len_out,
    ybuf,
    bbuf,
    sbuf,
    dbuf,
    ebuf,
    hbuf,
    gbuf,
    rbuf,
    cos_e,
    sin_e,
    wt_e,
    len_row,
    edge_in,
    edge_out,
    e_ybuf,
    e_cbuf,
    e_kbuf,
    e_bbuf,
    e_gbuf,
    e_hbuf,
    e_fbuf,
    e_rbuf,
    in_sem,
    send_sem,
    recv_sem,
    len_send,
    len_recv,
):
    p = lax.axis_index("pencil")
    s = lax.axis_index("slab")
    pairs = [
        (pair_hbm, pair_ref),
        (str_hbm, str_ref),
        (cent_hbm, cent_ref),
        (len_hbm, len_ref),
        (x_hbm, x_ref),
        (prop_hbm, prop_ref),
    ]
    inputs = [pltpu.make_async_copy(src, dst, in_sem.at[i]) for i, (src, dst) in enumerate(pairs)]
    for item in inputs:
        item.start()

    barrier = pltpu.get_barrier_semaphore()

    def far(n, size):
        half = (n + 1) // 2
        return size // 2 + (1 - 2 * (n % 2)) * half

    def pencil_peer(n):
        return lax.rem(p + far(n, NP), NP)

    def slab_peer(n):
        return lax.rem(s + far(n, NS), NS)

    @pl.loop(0, NP - 1)
    def _(n):
        pl.semaphore_signal(barrier, inc=1, device_id=(s, pencil_peer(n)), device_id_type=MESH)

    @pl.loop(0, NS - 1)
    def _(n):
        pl.semaphore_signal(barrier, inc=1, device_id=(slab_peer(n), p), device_id_type=MESH)

    def copy(src, dst, k, device):
        return pltpu.make_async_remote_copy(
            src_ref=src,
            dst_ref=dst,
            send_sem=send_sem.at[k],
            recv_sem=recv_sem.at[k],
            device_id=device,
            device_id_type=MESH,
        )

    def pencil_exchange(src, dst, chunk, k):
        @pl.loop(0, NP - 1)
        def _(n):
            q = pencil_peer(n)
            copy(src.at[chunk, q], dst.at[chunk, p], k, (s, q)).start()

        dst[chunk, pl.ds(p, 1)] = src[chunk, pl.ds(p, 1)]

    def slab_exchange(src, dst, chunk, k):
        @pl.loop(0, NS - 1)
        def _(n):
            q = slab_peer(n)
            copy(src.at[chunk, q], dst.at[chunk, s], k, (q, p)).start()

        dst[chunk, pl.ds(s, 1)] = src[chunk, pl.ds(s, 1)]

    def arrived(buf, chunk, k, count):
        part = buf.at[chunk, pl.ds(0, count - 1)]
        copy(part, part, k, (s, p)).wait_recv()

    def left(buf, chunk, k, count):
        part = buf.at[chunk, pl.ds(0, count - 1)]
        copy(part, part, k, (s, p)).wait_send()

    inputs[0].wait()
    inputs[1].wait()
    strength = str_ref[...]
    first, second = pair_ref[0:1, :], pair_ref[1:2, :]

    def hot_rows(labels):
        return (iota((N, 32), 0) % C == labels).astype(F32)

    def hot_cols(labels):
        shape = (32, 32)
        col = jnp.sum(jnp.where(iota(shape, 0) == iota(shape, 1), labels, 0), axis=1, keepdims=True)
        return (iota((32, N), 1) % C == col).astype(F32)

    rows_1, rows_2, cols_1, cols_2 = hot_rows(first), hot_rows(second), hot_cols(first), hot_cols(second)
    tiled = jnp.zeros((N, N), F32)
    for part in split3(strength):
        scale = part.astype(F32)
        tiled = tiled + jnp.dot((rows_1 * scale).astype(BF16), cols_2.astype(BF16), preferred_element_type=F32)
        tiled = tiled + jnp.dot((rows_2 * scale).astype(BF16), cols_1.astype(BF16), preferred_element_type=F32)
    row, col = iota((N, N), 0), iota((N, N), 1)
    kron_hi[...], kron_lo[...] = split2(jnp.where(row // C == col // C, tiled, 0.0))
    row, col = iota((128, 128), 0), iota((128, 128), 1)
    same = (row // C) % 4 == (col // C) % 4
    sign = (row // 64 - col // 64).astype(F32)
    mix_hi[...], mix_lo[...] = split2(jnp.where(same, tiled[:128, :128] * sign, 0.0))

    inputs[2].wait()
    inputs[3].wait()
    half = 0.5 * STEP
    cent = cent_ref[...]
    cent_col = [column(cent[e : e + 1], C) for e in range(3)]
    angle_1 = half * radial(iota((C, N), 1), cent_col[0])
    cos_1, sin_1 = jnp.cos(angle_1), jnp.sin(angle_1)
    lane = iota((C, 16), 1)
    angle_23 = half * (radial(L2 * p + lane % L2, cent_col[1]) + radial(L3 * s + lane // L2, cent_col[2]))
    cos_23, sin_23 = jnp.cos(angle_23), jnp.sin(angle_23)
    for m in range(16):
        c23, s23 = cos_23[:, m : m + 1], sin_23[:, m : m + 1]
        cos_a[m * C : (m + 1) * C] = cos_1 * c23 - sin_1 * s23
        sin_a[m * C : (m + 1) * C] = sin_1 * c23 + cos_1 * s23

    lens = len_ref[...].astype(F32)
    lane = iota((8, 128), 1)
    len_tile = jnp.zeros((8, 128), F32)
    len_rows = []
    for i3 in range(L3):
        col = column(lens[i3 : i3 + 1], L2)
        len_rows.append(col)
        edge_out[i3] = jnp.where(lane == p, col, jnp.zeros_like(col))
        len_tile = len_tile + jnp.where(lane == L3 * s + i3, col, jnp.zeros_like(col))
    len_out[0] = len_tile
    len_a = jnp.concatenate(len_rows, axis=0)

    row, col = iota((16, N), 0), iota((16, N), 1)
    farthest = jnp.maximum(jnp.maximum(L2 * p + row % L2, L3 * s + row // L2), col).astype(F32)
    live = (col.astype(F32) < len_a).astype(F32)
    lv_a[...] = live
    wl_a[...] = live * (half / (1.0 + 0.02 * farthest))

    inputs[4].wait()
    kron = (kron_hi[...], kron_lo[...])

    def potential(re, im):
        cosine, sine = cos_a[...], sin_a[...]
        turned_re = re * cosine + im * sine
        turned_im = im * cosine - re * sine
        mixed_re = product(kron, split2(turned_im))
        mixed_im = product(kron, split2(turned_re))

        def rows(a):
            return jnp.concatenate([jnp.broadcast_to(a[m : m + 1], (C, N)) for m in range(16)], axis=0)

        weight, alive = rows(wl_a[...]), rows(lv_a[...])
        return turned_re * alive + weight * mixed_re, turned_im * alive - weight * mixed_im

    def load(part):
        blocks = []
        for i3 in range(L3):
            for i2 in range(L2):
                base = (i2 * 2 + part) * 64 + i3
                blocks.append(
                    jnp.concatenate([x_ref[pl.ds(base + 2 * l, C, stride=4), :] for l in range(2)], axis=1)
                )
        return jnp.concatenate(blocks, axis=0)

    v_re, v_im = potential(load(0), load(1))
    u_hi[...], u_lo[...] = split2(jnp.concatenate([v_re, v_im], axis=1))
    u = (u_hi[...], u_lo[...])

    inputs[5].wait()
    sub = iota((1, 8, 2 * N), 1)

    def interleaved(re, im):
        top = jnp.concatenate([re, -im], axis=1).reshape(NP, 8, 2 * N)
        low = jnp.concatenate([im, re], axis=1).reshape(NP, 8, 2 * N)
        early = jnp.where(sub < 4, top, pltpu.roll(low, 4, 1))
        late = jnp.where(sub < 4, pltpu.roll(top, 4, 1), low)
        return [split2(v.reshape(N, 2 * N)) for v in (early, late)]

    for part, (high, low) in enumerate(interleaved(prop_ref[0], prop_ref[1])):
        w1_hi[part], w1_lo[part] = high, low

    def first_line(half_of):
        y = product((w1_hi[half_of], w1_lo[half_of]), u, ((1,), (1,)))
        return [y[:, i * 128 : (i + 1) * 128] for i in range(L3)]

    y = first_line(0)
    for i3 in range(L3):
        ybuf[0, :, i3] = y[i3].reshape(NP, 8, 128)

    root = s == p // 2

    def len_copy(src, dst, k, device):
        return pltpu.make_async_remote_copy(
            src_ref=src,
            dst_ref=dst,
            send_sem=len_send.at[k],
            recv_sem=len_recv.at[k],
            device_id=device,
            device_id_type=MESH,
        )

    pl.semaphore_wait(barrier, NP + NS - 2)

    @pl.when(jnp.logical_not(root))
    def _():
        len_copy(len_out.at[0], len_col.at[s], 0, (p // 2, p)).start()

    for i3 in range(L3):

        @pl.when(p != L3 * s + i3)
        def _():
            len_copy(edge_out.at[i3], len_row.at[p], 2 + i3, (s, L3 * s + i3)).start()

    pencil_exchange(ybuf, bbuf, 0, 0)

    y = first_line(1)
    for chunk in range(CHUNKS):
        for i3 in range(L3):
            e_ybuf[chunk, :, i3] = y[i3].reshape(NS, CHUNKS, 8, 128)[:, chunk]
        slab_exchange(e_ybuf, e_cbuf, chunk, 4 + chunk)

    @pl.when(root)
    def _():
        len_col[pl.ds(s, 1)] = len_out[pl.ds(0, 1)]
        part = len_col.at[pl.ds(0, NS - 1)]
        len_copy(part, part, 0, (s, p)).wait_recv()
        total = jnp.sum(len_col[...], axis=0)
        len_out[1] = total
        len_in[pl.ds(lax.rem(p, 2), 1)] = total[None]

        @pl.loop(0, NP - 1)
        def _(n):
            len_copy(len_out.at[1], len_in.at[lax.rem(p, 2)], 1, (s, pencil_peer(n))).start()

    def edge_third(x):
        g1 = band(x)
        g2 = band(g1)
        sign = jnp.where(iota((1, 8, 128), 1) < 4, 1.0, -1.0)
        return x + sign * pltpu.roll(g1, 4, 1) - 0.5 * g2

    def edge_1(chunk):
        arrived(e_cbuf, chunk, 4 + chunk, NS)
        e_kbuf[chunk] = edge_third(e_cbuf[chunk].reshape(NP, 8, 128))
        pencil_exchange(e_kbuf, e_bbuf, chunk, 6 + chunk)

    re, im = prop_ref[0], prop_ref[1]
    q2_hi[...], q2_lo[...] = split2(jnp.concatenate([re, im], axis=0))

    edge_1(0)
    edge_1(1)

    @pl.when(root)
    def _():
        len_row[pl.ds(p, 1)] = edge_out[pl.ds(lax.rem(p, 2), 1)]
        part = len_row.at[pl.ds(0, NP - 1)]
        len_copy(part, part, 2 + lax.rem(p, 2), (s, p)).wait_recv()
        total = jnp.sum(len_row[...], axis=0)
        edge_out[2] = total
        edge_in[0] = total

        @pl.loop(0, NS - 1)
        def _(n):
            len_copy(edge_out.at[2], edge_in.at[0], 4, (slab_peer(n), p)).start()

    for part, (high, low) in enumerate(interleaved(re.T, -im.T)):
        wf_hi[part], wf_lo[part] = high, low

    lane = iota((C, 128), 1)
    cent_row = [
        jnp.sum(jnp.where(iota((C, 128), 0) == lane % C, col, 0.0), axis=0, keepdims=True) for col in cent_col
    ]
    lane = iota((1, 128), 1)
    second_pos = 16 * s + iota((16, 128), 0)
    third_pos = iota((32, 128), 0)
    first_pos = 8 * p + (lane // C) % 4

    angle_2 = STEP * radial(second_pos, cent_row[1])
    angle_3 = STEP * radial(third_pos, cent_row[2])
    cos_3, sin_3 = jnp.cos(angle_3), jnp.sin(angle_3)
    turn = jnp.where(lane < 64, 1.0, -1.0)
    angle_12 = angle_2 + STEP * radial(first_pos, cent_row[0])
    cos_12, sin_12 = jnp.cos(angle_12), jnp.sin(angle_12)
    for i in range(32):
        c3, s3 = cos_3[i : i + 1], sin_3[i : i + 1]
        cos_d[i] = cos_12 * c3 - sin_12 * s3
        sin_d[i] = turn * (sin_12 * c3 + cos_12 * s3)

    angle_2 = STEP * radial(iota((N, 128), 0), cent_row[1])
    cos_2, sin_2 = jnp.cos(angle_2), jnp.sin(angle_2)
    edge_rows = iota((N, 128), 0)

    def edge_first_pos(chunk):
        return 8 * (CHUNKS * s + chunk) + 4 + (lane // C) % 4

    for chunk in range(CHUNKS):
        position = edge_first_pos(chunk)
        angle_13 = STEP * (radial(position, cent_row[0]) + radial(jnp.full((1, 128), p, jnp.int32), cent_row[2]))
        cos_13, sin_13 = jnp.cos(angle_13), jnp.sin(angle_13)
        cos_e[chunk] = cos_2 * cos_13 - sin_2 * sin_13
        sin_e[chunk] = turn * (sin_2 * cos_13 + cos_2 * sin_13)
        farthest = jnp.maximum(jnp.maximum(edge_rows, position), p).astype(F32)
        wt_e[chunk] = STEP / (1.0 + 0.02 * farthest)

    q2 = (q2_hi[...], q2_lo[...])

    def second_line(z):
        both = product(q2, split2(z))
        return both[:N] - turn * pltpu.roll(both[N:], 64, 1)

    def third_line(psi):
        g1 = band(psi)
        g2 = band(g1)
        return psi + turn * pltpu.roll(g1, 64, 2) - 0.5 * g2

    def third_potential(psi):
        turned = psi * cos_d[...] + sin_d[...] * pltpu.roll(psi, 64, 2)
        mixed = product(split2(turned.reshape(512, 128)), (mix_hi[...], mix_lo[...])).reshape(32, 16, 128)
        both = jnp.maximum(second_pos, first_pos)
        lengths = jnp.concatenate([len_in[0], len_in[1]], axis=0)
        out = []
        for i in range(32):
            weight = STEP / (1.0 + 0.02 * jnp.maximum(both, i).astype(F32))
            alive = first_pos.astype(F32) < lengths[:, i : i + 1]
            out.append(jnp.where(alive, turned[i] + weight * mixed[i], 0.0))
        return jnp.stack(out, axis=0)

    def second_pair(z):
        both = product(q2, split2(jnp.concatenate(z, axis=1)))
        both = [both[:, i * 128 : (i + 1) * 128] for i in range(L3)]
        return [b[:N] - turn * pltpu.roll(b[N:], 64, 1) for b in both]

    def step_1():
        arrived(bbuf, 0, 0, NP)
        z = second_pair([flip_blocks(bbuf[0, :, i3]).reshape(N, 128) for i3 in range(L3)])
        for i3 in range(L3):
            sbuf[0, :, i3] = z[i3].reshape(NS, 16, 128)
        slab_exchange(sbuf, dbuf, 0, 1)

    def step_2():
        arrived(dbuf, 0, 1, NS)
        psi = third_line(dbuf[0].reshape(32, 16, 128))
        ebuf[0] = third_line(third_potential(psi)).reshape(NS, L3, 16, 128)
        slab_exchange(ebuf, hbuf, 0, 2)

    def step_3():
        arrived(hbuf, 0, 2, NS)
        z = second_pair([hbuf[0, :, i3].reshape(N, 128) for i3 in range(L3)])
        for i3 in range(L3):
            gbuf[0, :, i3] = flip_blocks(z[i3].reshape(NP, 8, 128))
        pencil_exchange(gbuf, rbuf, 0, 3)

    def edge_potential(psi, chunk):
        turned = psi * cos_e[chunk] + sin_e[chunk] * pltpu.roll(psi, 64, 1)
        mixed = product(split2(turned), (mix_hi[...], mix_lo[...]))
        lengths = edge_in[0]
        end = jnp.concatenate([jnp.broadcast_to(lengths[:, i : i + 1], (8, 128)) for i in range(NP)], axis=0)
        return jnp.where(edge_first_pos(chunk).astype(F32) < end, turned + wt_e[chunk] * mixed, 0.0)

    def edge_2(chunk):
        arrived(e_bbuf, chunk, 6 + chunk, NP)
        z = second_line(flip_blocks(e_bbuf[chunk]).reshape(N, 128))
        z = second_line(edge_potential(z, chunk))
        e_gbuf[chunk] = flip_blocks(z.reshape(NP, 8, 128))
        pencil_exchange(e_gbuf, e_hbuf, chunk, 8 + chunk)

    def edge_3(chunk):
        arrived(e_hbuf, chunk, 8 + chunk, NP)
        e_fbuf[chunk] = edge_third(e_hbuf[chunk]).reshape(NS, L3, 8, 128)
        slab_exchange(e_fbuf, e_rbuf, chunk, 10 + chunk)

    step_1()

    @pl.when(root)
    def _():
        len_copy(len_in.at[0], len_in.at[0], 1, (s, p)).wait_recv()

    @pl.when(jnp.logical_not(root))
    def _():
        len_copy(len_in, len_in, 1, (s, p)).wait_recv()
        len_copy(edge_in, edge_in, 4, (s, p)).wait_recv()

    edge_2(0)
    step_2()
    edge_2(1)
    step_3()

    edge_3(0)
    edge_3(1)
    for chunk in range(CHUNKS):
        arrived(e_rbuf, chunk, 10 + chunk, NS)
    r = [jnp.stack([e_rbuf[chunk, :, i3] for chunk in range(CHUNKS)], axis=1).reshape(N, 128) for i3 in range(L3)]
    out = product(split2(jnp.concatenate(r, axis=1).T), (wf_hi[1], wf_lo[1]))
    arrived(rbuf, 0, 3, NP)
    r = jnp.concatenate([rbuf[0, :, i3].reshape(N, 128) for i3 in range(L3)], axis=1)
    out = out + product(split2(r.T), (wf_hi[0], wf_lo[0]))

    out = potential(out[:, :N], out[:, N:])
    for part in range(2):
        for i3 in range(L3):
            for i2 in range(L2):
                base = (i2 * 2 + part) * 64 + i3
                start = (i3 * L2 + i2) * C
                for l in range(2):
                    o_ref[pl.ds(base + 2 * l, C, stride=4), :] = out[part][start : start + C, l * 128 : (l + 1) * 128]

    left(ybuf, 0, 0, NP)
    left(sbuf, 0, 1, NS)
    left(ebuf, 0, 2, NS)
    left(gbuf, 0, 3, NP)
    for chunk in range(CHUNKS):
        left(e_ybuf, chunk, 4 + chunk, NS)
        left(e_kbuf, chunk, 6 + chunk, NP)
        left(e_gbuf, chunk, 8 + chunk, NP)
        left(e_fbuf, chunk, 10 + chunk, NS)

    @pl.when(root)
    def _():
        @pl.loop(0, NP - 1)
        def _(n):
            len_copy(len_out.at[1], len_in.at[0], 1, (s, p)).wait_send()

        @pl.loop(0, NS - 1)
        def _(n):
            len_copy(edge_out.at[2], edge_in.at[0], 4, (s, p)).wait_send()

    @pl.when(jnp.logical_not(root))
    def _():
        len_copy(len_out.at[0], len_col.at[0], 0, (s, p)).wait_send()

    for i3 in range(L3):

        @pl.when(p != L3 * s + i3)
        def _():
            len_copy(edge_out.at[i3], len_row.at[0], 2 + i3, (s, p)).wait_send()


def on_device(wavefunction, propagator, lengths, centrifugal, channel_pairs, strengths):
    shape = wavefunction.shape
    x = wavefunction.reshape(8, 2, 16, 2, 2, 128).transpose(0, 1, 2, 4, 3, 5).reshape(1024, 128)
    operands = (x, propagator, lengths, centrifugal, channel_pairs.T, strengths.reshape(1, 32))

    def vmem(*dims, dtype=F32):
        return pltpu.VMEM(dims, dtype)

    scratch = [pltpu.VMEM(a.shape, a.dtype) for a in operands]
    scratch += [
        vmem(N, N),
        vmem(N, N),
        vmem(16, N),
        vmem(16, N),
        vmem(N, N, dtype=BF16),
        vmem(N, N, dtype=BF16),
        vmem(128, 128, dtype=BF16),
        vmem(128, 128, dtype=BF16),
        vmem(2, N, 2 * N, dtype=BF16),
        vmem(2, N, 2 * N, dtype=BF16),
        vmem(2 * N, N, dtype=BF16),
        vmem(2 * N, N, dtype=BF16),
        vmem(2, N, 2 * N, dtype=BF16),
        vmem(2, N, 2 * N, dtype=BF16),
        vmem(32, 16, 128),
        vmem(32, 16, 128),
        vmem(N, 2 * N, dtype=BF16),
        vmem(N, 2 * N, dtype=BF16),
        vmem(NS, 8, 128),
        vmem(2, 8, 128),
        vmem(2, 8, 128),
        vmem(1, NP, L3, 8, 128),
        vmem(1, NP, L3, 8, 128),
        vmem(1, NS, L3, 16, 128),
        vmem(1, NS, L3, 16, 128),
        vmem(1, NS, L3, 16, 128),
        vmem(1, NS, L3, 16, 128),
        vmem(1, NP, L3, 8, 128),
        vmem(1, NP, L3, 8, 128),
        vmem(CHUNKS, N, 128),
        vmem(CHUNKS, N, 128),
        vmem(CHUNKS, N, 128),
        vmem(NP, 8, 128),
        vmem(1, 8, 128),
        vmem(3, 8, 128),
        vmem(CHUNKS, NS, L3, 8, 128),
        vmem(CHUNKS, NS, L3, 8, 128),
        vmem(CHUNKS, NP, 8, 128),
        vmem(CHUNKS, NP, 8, 128),
        vmem(CHUNKS, NP, 8, 128),
        vmem(CHUNKS, NP, 8, 128),
        vmem(CHUNKS, NS, L3, 8, 128),
        vmem(CHUNKS, NS, L3, 8, 128),
        pltpu.SemaphoreType.DMA((6,)),
        pltpu.SemaphoreType.DMA((12,)),
        pltpu.SemaphoreType.DMA((12,)),
        pltpu.SemaphoreType.DMA((5,)),
        pltpu.SemaphoreType.DMA((5,)),
    ]
    out = pl.pallas_call(
        body,
        out_shape=jax.ShapeDtypeStruct((1024, 128), F32),
        in_specs=[pl.BlockSpec(memory_space=pltpu.HBM)] * 6,
        out_specs=pl.BlockSpec(memory_space=pltpu.VMEM),
        scratch_shapes=scratch,
        compiler_params=pltpu.CompilerParams(
            collective_id=0, has_side_effects=True, vmem_limit_bytes=53 * 2**20
        ),
        name="propagate",
    )(*operands)
    return out.reshape(8, 2, 16, 2, 2, 128).transpose(0, 1, 2, 4, 3, 5).reshape(shape)


def solution(mesh):
    in_specs = (P("pencil", None, None, "slab", None), P(), P("slab", "pencil"), P(), P(), P())
    out_specs = P("pencil", None, None, "slab", None)
    return jax.shard_map(
        on_device, mesh=mesh, in_specs=in_specs, out_specs=out_specs, check_vma=False
    )
```

```python
import jax
import jax.numpy as jnp
from jax import lax
from jax.experimental import pallas as pl
from jax.experimental.pallas import tpu as pltpu
from jax.sharding import PartitionSpec as P


MESH = pl.DeviceIdType.MESH
F32 = jnp.float32
BF16 = jnp.bfloat16
STEP = 0.1
GRID = 0.5
CHARGE = 3.0
BAND = 0.3
NP = 32
NS = 16
L2 = 8
L3 = 2
C = 16
N = 256
CHUNKS = 2


def iota(shape, dim):
    return lax.broadcasted_iota(jnp.int32, shape, dim)


def split2(x):
    high = x.astype(BF16)
    return high, (x - high.astype(F32)).astype(BF16)


def split3(x):
    high = x.astype(BF16)
    rest = x - high.astype(F32)
    middle = rest.astype(BF16)
    return high, middle, (rest - middle.astype(F32)).astype(BF16)


def product(a, b, contract=((1,), (0,))):
    def one(x, y):
        return lax.dot_general(x, y, (contract, ((), ())), preferred_element_type=F32)

    return one(a[0], b[0]) + (one(a[0], b[1]) + one(a[1], b[0]))


def column(row, count):
    shape = (count, row.shape[1])
    return jnp.sum(jnp.where(iota(shape, 0) == iota(shape, 1), row, jnp.zeros_like(row)), axis=1, keepdims=True)


def radial(position, weight):
    radius = GRID * (position.astype(F32) + 1.0)
    return -CHARGE / radius + weight / (radius * radius)


def flip_blocks(x):
    row, group = iota((1, 8, 128), 1), iota((1, 8, 128), 2) // 16
    for bit in (4, 2, 1):
        lanes = 16 * bit
        has_row, has_group = (row // bit) % 2, (group // bit) % 2
        down = pltpu.roll(pltpu.roll(x, bit, 1), 128 - lanes, 2)
        if bit == 4:
            up = down
        else:
            up = pltpu.roll(pltpu.roll(x, 8 - bit, 1), lanes, 2)
        x = jnp.where(has_row == has_group, x, jnp.where(has_row == 1, down, up))
    return x


def band(x):
    zero = jnp.zeros((2,) + x.shape[1:], F32)
    y = jnp.concatenate([zero, x, zero], axis=0)
    return (BAND / 24.0) * (y[:32] + y[4:36] - 16.0 * (y[1:33] + y[3:35]) + 30.0 * x)


def body(
    x_hbm,
    prop_hbm,
    len_hbm,
    cent_hbm,
    pair_hbm,
    str_hbm,
    o_ref,
    x_ref,
    prop_ref,
    len_ref,
    cent_ref,
    pair_ref,
    str_ref,
    cos_a,
    sin_a,
    wl_a,
    lv_a,
    kron_hi,
    kron_lo,
    mix,
    w1_hi,
    w1_lo,
    q2_hi,
    q2_lo,
    wf_hi,
    wf_lo,
    cos_d,
    sin_d,
    u_hi,
    u_lo,
    len_col,
    len_in,
    len_out,
    ybuf,
    bbuf,
    sbuf,
    dbuf,
    ebuf,
    hbuf,
    gbuf,
    rbuf,
    cos_e,
    sin_e,
    wt_e,
    len_row,
    edge_in,
    edge_out,
    e_ybuf,
    e_cbuf,
    e_kbuf,
    e_bbuf,
    e_gbuf,
    e_hbuf,
    e_fbuf,
    e_rbuf,
    in_sem,
    send_sem,
    recv_sem,
    len_send,
    len_recv,
):
    p = lax.axis_index("pencil")
    s = lax.axis_index("slab")
    barrier = pltpu.get_barrier_semaphore()

    def far(n, size):
        half = (n + 1) // 2
        return size // 2 + (1 - 2 * (n % 2)) * half

    def pencil_peer(n):
        return lax.rem(p + far(n, NP), NP)

    def slab_peer(n):
        return lax.rem(s + far(n, NS), NS)

    @pl.loop(0, NP - 1)
    def _(n):
        pl.semaphore_signal(barrier, inc=1, device_id=(s, pencil_peer(n)), device_id_type=MESH)

    @pl.loop(0, NS - 1)
    def _(n):
        pl.semaphore_signal(barrier, inc=1, device_id=(slab_peer(n), p), device_id_type=MESH)

    pairs = [
        (pair_hbm, pair_ref),
        (str_hbm, str_ref),
        (cent_hbm, cent_ref),
        (len_hbm, len_ref),
        (x_hbm, x_ref),
        (prop_hbm, prop_ref),
    ]
    inputs = [pltpu.make_async_copy(src, dst, in_sem.at[i]) for i, (src, dst) in enumerate(pairs)]
    for item in inputs:
        item.start()

    def copy(src, dst, k, device):
        return pltpu.make_async_remote_copy(
            src_ref=src,
            dst_ref=dst,
            send_sem=send_sem.at[k],
            recv_sem=recv_sem.at[k],
            device_id=device,
            device_id_type=MESH,
        )

    def pencil_exchange(src, dst, chunk, k):
        @pl.loop(0, NP - 1)
        def _(n):
            q = pencil_peer(n)
            copy(src.at[chunk, q], dst.at[chunk, p], k, (s, q)).start()

        dst[chunk, pl.ds(p, 1)] = src[chunk, pl.ds(p, 1)]

    def slab_exchange(src, dst, chunk, k):
        @pl.loop(0, NS - 1)
        def _(n):
            q = slab_peer(n)
            copy(src.at[chunk, q], dst.at[chunk, s], k, (q, p)).start()

        dst[chunk, pl.ds(s, 1)] = src[chunk, pl.ds(s, 1)]

    def arrived(buf, chunk, k, count):
        part = buf.at[chunk, pl.ds(0, count - 1)]
        copy(part, part, k, (s, p)).wait_recv()

    def left(buf, chunk, k, count):
        part = buf.at[chunk, pl.ds(0, count - 1)]
        copy(part, part, k, (s, p)).wait_send()

    inputs[0].wait()
    inputs[1].wait()
    strength = str_ref[...]
    first, second = pair_ref[0:1, :], pair_ref[1:2, :]

    def hot_rows(labels):
        return (iota((N, 32), 0) % C == labels).astype(F32)

    def hot_cols(labels):
        shape = (32, 32)
        col = jnp.sum(jnp.where(iota(shape, 0) == iota(shape, 1), labels, 0), axis=1, keepdims=True)
        return (iota((32, N), 1) % C == col).astype(F32)

    rows_1, rows_2, cols_1, cols_2 = hot_rows(first), hot_rows(second), hot_cols(first), hot_cols(second)
    tiled = jnp.zeros((N, N), F32)
    for part in split3(strength):
        scale = part.astype(F32)
        tiled = tiled + jnp.dot((rows_1 * scale).astype(BF16), cols_2.astype(BF16), preferred_element_type=F32)
        tiled = tiled + jnp.dot((rows_2 * scale).astype(BF16), cols_1.astype(BF16), preferred_element_type=F32)
    row, col = iota((N, N), 0), iota((N, N), 1)
    kron_hi[...], kron_lo[...] = split2(jnp.where(row // C == col // C, tiled, 0.0))
    row, col = iota((128, 128), 0), iota((128, 128), 1)
    same = (row // C) % 4 == (col // C) % 4
    sign = (row // 64 - col // 64).astype(F32)
    high, low = split2(jnp.where(same, tiled[:128, :128] * sign, 0.0))
    mix[:128, :128], mix[:128, 128:] = high, low
    mix[128:, :128], mix[128:, 128:] = high, jnp.zeros_like(low)

    inputs[2].wait()
    inputs[3].wait()
    half = 0.5 * STEP
    cent = cent_ref[...]
    cent_col = [column(cent[e : e + 1], C) for e in range(3)]
    angle_1 = half * radial(iota((C, N), 1), cent_col[0])
    cos_1, sin_1 = jnp.cos(angle_1), jnp.sin(angle_1)
    lane = iota((C, 16), 1)
    angle_23 = half * (radial(L2 * p + lane % L2, cent_col[1]) + radial(L3 * s + lane // L2, cent_col[2]))
    cos_23, sin_23 = jnp.cos(angle_23), jnp.sin(angle_23)
    for m in range(16):
        c23, s23 = cos_23[:, m : m + 1], sin_23[:, m : m + 1]
        cos_a[m * C : (m + 1) * C] = cos_1 * c23 - sin_1 * s23
        sin_a[m * C : (m + 1) * C] = sin_1 * c23 + cos_1 * s23

    lens = len_ref[...].astype(F32)
    lane = iota((8, 128), 1)
    len_tile = jnp.zeros((8, 128), F32)
    len_rows = []
    for i3 in range(L3):
        col = column(lens[i3 : i3 + 1], L2)
        len_rows.append(col)
        edge_out[i3] = jnp.where(lane == p, col, jnp.zeros_like(col))
        len_tile = len_tile + jnp.where(lane == L3 * s + i3, col, jnp.zeros_like(col))
    len_out[0] = len_tile
    len_a = jnp.concatenate(len_rows, axis=0)

    row, col = iota((16, N), 0), iota((16, N), 1)
    farthest = jnp.maximum(jnp.maximum(L2 * p + row % L2, L3 * s + row // L2), col).astype(F32)
    live = (col.astype(F32) < len_a).astype(F32)
    lv_a[...] = live
    wl_a[...] = live * (half / (1.0 + 0.02 * farthest))

    inputs[4].wait()
    kron = (kron_hi[...], kron_lo[...])

    def potential(re, im, kron, start, count):
        rows_of = slice(start * C, (start + count) * C)
        cosine, sine = cos_a[rows_of], sin_a[rows_of]
        turned_re = re * cosine + im * sine
        turned_im = im * cosine - re * sine
        mixed_re = product(kron, split2(turned_im))
        mixed_im = product(kron, split2(turned_re))

        def rows(a):
            return jnp.concatenate([jnp.broadcast_to(a[m : m + 1], (C, N)) for m in range(start, start + count)], axis=0)

        weight, alive = rows(wl_a[...]), rows(lv_a[...])
        return turned_re * alive + weight * mixed_re, turned_im * alive - weight * mixed_im

    def load(part):
        blocks = []
        for i3 in range(L3):
            for i2 in range(L2):
                base = (i2 * 2 + part) * 64 + i3
                blocks.append(
                    jnp.concatenate([x_ref[pl.ds(base + 2 * l, C, stride=4), :] for l in range(2)], axis=1)
                )
        return jnp.concatenate(blocks, axis=0)

    v_re, v_im = potential(load(0), load(1), kron, 0, 16)
    u_hi[...], u_lo[...] = split2(jnp.concatenate([v_re, v_im], axis=1))
    u = (u_hi[...], u_lo[...])

    inputs[5].wait()
    sub = iota((1, 8, 2 * N), 1)

    def interleaved(re, im):
        top = jnp.concatenate([re, -im], axis=1).reshape(NP, 8, 2 * N)
        low = jnp.concatenate([im, re], axis=1).reshape(NP, 8, 2 * N)
        early = jnp.where(sub < 4, top, pltpu.roll(low, 4, 1))
        late = jnp.where(sub < 4, pltpu.roll(top, 4, 1), low)
        return [split2(v.reshape(N, 2 * N)) for v in (early, late)]

    for part, (high, low) in enumerate(interleaved(prop_ref[0], prop_ref[1])):
        w1_hi[part], w1_lo[part] = high, low

    def first_line(half_of):
        y = product((w1_hi[half_of], w1_lo[half_of]), u, ((1,), (1,)))
        return [y[:, i * 128 : (i + 1) * 128] for i in range(L3)]

    y = first_line(0)
    for i3 in range(L3):
        ybuf[0, :, i3] = y[i3].reshape(NP, 8, 128)

    root = s == p // 2

    def len_copy(src, dst, k, device):
        return pltpu.make_async_remote_copy(
            src_ref=src,
            dst_ref=dst,
            send_sem=len_send.at[k],
            recv_sem=len_recv.at[k],
            device_id=device,
            device_id_type=MESH,
        )

    pl.semaphore_wait(barrier, NP + NS - 2)

    @pl.when(jnp.logical_not(root))
    def _():
        len_copy(len_out.at[0], len_col.at[s], 0, (p // 2, p)).start()

    for i3 in range(L3):

        @pl.when(p != L3 * s + i3)
        def _():
            len_copy(edge_out.at[i3], len_row.at[p], 2 + i3, (s, L3 * s + i3)).start()

    pencil_exchange(ybuf, bbuf, 0, 0)

    y = first_line(1)
    for chunk in range(CHUNKS):
        for i3 in range(L3):
            e_ybuf[chunk, :, i3] = y[i3].reshape(NS, CHUNKS, 8, 128)[:, chunk]
        slab_exchange(e_ybuf, e_cbuf, chunk, 4 + chunk)

    @pl.when(root)
    def _():
        len_col[pl.ds(s, 1)] = len_out[pl.ds(0, 1)]
        part = len_col.at[pl.ds(0, NS - 1)]
        len_copy(part, part, 0, (s, p)).wait_recv()
        total = jnp.sum(len_col[...], axis=0)
        len_out[1] = total
        len_in[pl.ds(lax.rem(p, 2), 1)] = total[None]

        @pl.loop(0, NP - 1)
        def _(n):
            len_copy(len_out.at[1], len_in.at[lax.rem(p, 2)], 1, (s, pencil_peer(n))).start()

    def edge_third(x):
        g1 = band(x)
        g2 = band(g1)
        sign = jnp.where(iota((1, 8, 128), 1) < 4, 1.0, -1.0)
        return x + sign * pltpu.roll(g1, 4, 1) - 0.5 * g2

    def edge_1(chunk):
        arrived(e_cbuf, chunk, 4 + chunk, NS)
        e_kbuf[chunk] = edge_third(e_cbuf[chunk].reshape(NP, 8, 128))
        pencil_exchange(e_kbuf, e_bbuf, chunk, 6 + chunk)

    re, im = prop_ref[0], prop_ref[1]
    q2_hi[...], q2_lo[...] = split2(jnp.concatenate([re, im], axis=0))

    edge_1(0)
    edge_1(1)

    @pl.when(root)
    def _():
        len_row[pl.ds(p, 1)] = edge_out[pl.ds(lax.rem(p, 2), 1)]
        part = len_row.at[pl.ds(0, NP - 1)]
        len_copy(part, part, 2 + lax.rem(p, 2), (s, p)).wait_recv()
        total = jnp.sum(len_row[...], axis=0)
        edge_out[2] = total
        edge_in[0] = total

        @pl.loop(0, NS - 1)
        def _(n):
            len_copy(edge_out.at[2], edge_in.at[0], 4, (slab_peer(n), p)).start()

    for part, (high, low) in enumerate(interleaved(re.T, -im.T)):
        wf_hi[part], wf_lo[part] = high, low

    lane = iota((C, 128), 1)
    cent_row = [
        jnp.sum(jnp.where(iota((C, 128), 0) == lane % C, col, 0.0), axis=0, keepdims=True) for col in cent_col
    ]
    lane = iota((1, 128), 1)
    second_pos = 16 * s + iota((16, 128), 0)
    third_pos = iota((32, 128), 0)
    first_pos = 8 * p + (lane // C) % 4

    angle_2 = STEP * radial(second_pos, cent_row[1])
    angle_3 = STEP * radial(third_pos, cent_row[2])
    cos_3, sin_3 = jnp.cos(angle_3), jnp.sin(angle_3)
    turn = jnp.where(lane < 64, 1.0, -1.0)
    angle_12 = angle_2 + STEP * radial(first_pos, cent_row[0])
    cos_12, sin_12 = jnp.cos(angle_12), jnp.sin(angle_12)
    for i in range(32):
        c3, s3 = cos_3[i : i + 1], sin_3[i : i + 1]
        cos_d[i] = cos_12 * c3 - sin_12 * s3
        sin_d[i] = turn * (sin_12 * c3 + cos_12 * s3)

    angle_2 = STEP * radial(iota((N, 128), 0), cent_row[1])
    cos_2, sin_2 = jnp.cos(angle_2), jnp.sin(angle_2)
    edge_rows = iota((N, 128), 0)

    def edge_first_pos(chunk):
        return 8 * (CHUNKS * s + chunk) + 4 + (lane // C) % 4

    for chunk in range(CHUNKS):
        position = edge_first_pos(chunk)
        angle_13 = STEP * (radial(position, cent_row[0]) + radial(jnp.full((1, 128), p, jnp.int32), cent_row[2]))
        cos_13, sin_13 = jnp.cos(angle_13), jnp.sin(angle_13)
        cos_e[chunk] = cos_2 * cos_13 - sin_2 * sin_13
        sin_e[chunk] = turn * (sin_2 * cos_13 + cos_2 * sin_13)
        farthest = jnp.maximum(jnp.maximum(edge_rows, position), p).astype(F32)
        wt_e[chunk] = STEP / (1.0 + 0.02 * farthest)

    q2 = (q2_hi[...], q2_lo[...])

    def second_line(z):
        high, low = split2(z)
        both = jnp.dot(q2[0], jnp.concatenate([high, low], axis=1), preferred_element_type=F32)
        both = both[:, :128] + both[:, 128:] + jnp.dot(q2[1], high, preferred_element_type=F32)
        return both[:N] - turn * pltpu.roll(both[N:], 64, 1)

    def mixture(turned):
        both = jnp.dot(jnp.concatenate(split2(turned), axis=1), mix[...], preferred_element_type=F32)
        return both[:, :128] + both[:, 128:]

    def third_line(psi):
        g1 = band(psi)
        g2 = band(g1)
        return psi + turn * pltpu.roll(g1, 64, 2) - 0.5 * g2

    def third_potential(psi):
        turned = psi * cos_d[...] + sin_d[...] * pltpu.roll(psi, 64, 2)
        mixed = mixture(turned.reshape(512, 128)).reshape(32, 16, 128)
        both = jnp.maximum(second_pos, first_pos)
        lengths = jnp.concatenate([len_in[0], len_in[1]], axis=0)
        out = []
        for i in range(32):
            weight = STEP / (1.0 + 0.02 * jnp.maximum(both, i).astype(F32))
            alive = first_pos.astype(F32) < lengths[:, i : i + 1]
            out.append(jnp.where(alive, turned[i] + weight * mixed[i], 0.0))
        return jnp.stack(out, axis=0)

    def second_pair(z):
        both = product(q2, split2(jnp.concatenate(z, axis=1)))
        both = [both[:, i * 128 : (i + 1) * 128] for i in range(L3)]
        return [b[:N] - turn * pltpu.roll(b[N:], 64, 1) for b in both]

    def step_1():
        arrived(bbuf, 0, 0, NP)
        z = second_pair([flip_blocks(bbuf[0, :, i3]).reshape(N, 128) for i3 in range(L3)])
        for i3 in range(L3):
            sbuf[0, :, i3] = z[i3].reshape(NS, 16, 128)
        slab_exchange(sbuf, dbuf, 0, 1)

    def step_2():
        arrived(dbuf, 0, 1, NS)
        psi = third_line(dbuf[0].reshape(32, 16, 128))
        ebuf[0] = third_line(third_potential(psi)).reshape(NS, L3, 16, 128)
        slab_exchange(ebuf, hbuf, 0, 2)

    def step_3():
        arrived(hbuf, 0, 2, NS)
        z = second_pair([hbuf[0, :, i3].reshape(N, 128) for i3 in range(L3)])
        for i3 in range(L3):
            gbuf[0, :, i3] = flip_blocks(z[i3].reshape(NP, 8, 128))
        pencil_exchange(gbuf, rbuf, 0, 3)

    def edge_potential(psi, chunk):
        turned = psi * cos_e[chunk] + sin_e[chunk] * pltpu.roll(psi, 64, 1)
        mixed = mixture(turned)
        lengths = edge_in[0]
        end = jnp.concatenate([jnp.broadcast_to(lengths[:, i : i + 1], (8, 128)) for i in range(NP)], axis=0)
        return jnp.where(edge_first_pos(chunk).astype(F32) < end, turned + wt_e[chunk] * mixed, 0.0)

    def edge_2(chunk):
        arrived(e_bbuf, chunk, 6 + chunk, NP)
        z = second_line(flip_blocks(e_bbuf[chunk]).reshape(N, 128))
        z = second_line(edge_potential(z, chunk))
        e_gbuf[chunk] = flip_blocks(z.reshape(NP, 8, 128))
        pencil_exchange(e_gbuf, e_hbuf, chunk, 8 + chunk)

    def edge_3(chunk):
        arrived(e_hbuf, chunk, 8 + chunk, NP)
        e_fbuf[chunk] = edge_third(e_hbuf[chunk]).reshape(NS, L3, 8, 128)
        slab_exchange(e_fbuf, e_rbuf, chunk, 10 + chunk)

    step_1()

    @pl.when(root)
    def _():
        len_copy(len_in.at[0], len_in.at[0], 1, (s, p)).wait_recv()

    @pl.when(jnp.logical_not(root))
    def _():
        len_copy(len_in, len_in, 1, (s, p)).wait_recv()
        len_copy(edge_in, edge_in, 4, (s, p)).wait_recv()

    edge_2(0)
    step_2()
    edge_2(1)
    step_3()

    edge_3(0)
    edge_3(1)
    for chunk in range(CHUNKS):
        arrived(e_rbuf, chunk, 10 + chunk, NS)
    r = [jnp.stack([e_rbuf[chunk, :, i3] for chunk in range(CHUNKS)], axis=1).reshape(N, 128) for i3 in range(L3)]
    wf = [(wf_hi[k], wf_lo[k]) for k in range(2)]
    early = [product(split2(a.T), wf[1]) for a in r]
    arrived(rbuf, 0, 3, NP)
    block = (kron_hi[:128, :128], kron_lo[:128, :128])
    for i3 in range(L3):
        out = early[i3] + product(split2(rbuf[0, :, i3].reshape(N, 128).T), wf[0])
        out = potential(out[:, :N], out[:, N:], block, i3 * L2, L2)
        for part in range(2):
            for i2 in range(L2):
                base = (i2 * 2 + part) * 64 + i3
                for l in range(2):
                    o_ref[pl.ds(base + 2 * l, C, stride=4), :] = out[part][i2 * C : (i2 + 1) * C, l * 128 : (l + 1) * 128]

    left(ybuf, 0, 0, NP)
    left(sbuf, 0, 1, NS)
    left(ebuf, 0, 2, NS)
    left(gbuf, 0, 3, NP)
    for chunk in range(CHUNKS):
        left(e_ybuf, chunk, 4 + chunk, NS)
        left(e_kbuf, chunk, 6 + chunk, NP)
        left(e_gbuf, chunk, 8 + chunk, NP)
        left(e_fbuf, chunk, 10 + chunk, NS)

    @pl.when(root)
    def _():
        @pl.loop(0, NP - 1)
        def _(n):
            len_copy(len_out.at[1], len_in.at[0], 1, (s, p)).wait_send()

        @pl.loop(0, NS - 1)
        def _(n):
            len_copy(edge_out.at[2], edge_in.at[0], 4, (s, p)).wait_send()

    @pl.when(jnp.logical_not(root))
    def _():
        len_copy(len_out.at[0], len_col.at[0], 0, (s, p)).wait_send()

    for i3 in range(L3):

        @pl.when(p != L3 * s + i3)
        def _():
            len_copy(edge_out.at[i3], len_row.at[0], 2 + i3, (s, p)).wait_send()


def on_device(wavefunction, propagator, lengths, centrifugal, channel_pairs, strengths):
    shape = wavefunction.shape
    x = wavefunction.reshape(8, 2, 16, 2, 2, 128).transpose(0, 1, 2, 4, 3, 5).reshape(1024, 128)
    operands = (x, propagator, lengths, centrifugal, channel_pairs.T, strengths.reshape(1, 32))

    def vmem(*dims, dtype=F32):
        return pltpu.VMEM(dims, dtype)

    scratch = [pltpu.VMEM(a.shape, a.dtype) for a in operands]
    scratch += [
        vmem(N, N),
        vmem(N, N),
        vmem(16, N),
        vmem(16, N),
        vmem(N, N, dtype=BF16),
        vmem(N, N, dtype=BF16),
        vmem(N, N, dtype=BF16),
        vmem(2, N, 2 * N, dtype=BF16),
        vmem(2, N, 2 * N, dtype=BF16),
        vmem(2 * N, N, dtype=BF16),
        vmem(2 * N, N, dtype=BF16),
        vmem(2, N, 2 * N, dtype=BF16),
        vmem(2, N, 2 * N, dtype=BF16),
        vmem(32, 16, 128),
        vmem(32, 16, 128),
        vmem(N, 2 * N, dtype=BF16),
        vmem(N, 2 * N, dtype=BF16),
        vmem(NS, 8, 128),
        vmem(2, 8, 128),
        vmem(2, 8, 128),
        vmem(1, NP, L3, 8, 128),
        vmem(1, NP, L3, 8, 128),
        vmem(1, NS, L3, 16, 128),
        vmem(1, NS, L3, 16, 128),
        vmem(1, NS, L3, 16, 128),
        vmem(1, NS, L3, 16, 128),
        vmem(1, NP, L3, 8, 128),
        vmem(1, NP, L3, 8, 128),
        vmem(CHUNKS, N, 128),
        vmem(CHUNKS, N, 128),
        vmem(CHUNKS, N, 128),
        vmem(NP, 8, 128),
        vmem(1, 8, 128),
        vmem(3, 8, 128),
        vmem(CHUNKS, NS, L3, 8, 128),
        vmem(CHUNKS, NS, L3, 8, 128),
        vmem(CHUNKS, NP, 8, 128),
        vmem(CHUNKS, NP, 8, 128),
        vmem(CHUNKS, NP, 8, 128),
        vmem(CHUNKS, NP, 8, 128),
        vmem(CHUNKS, NS, L3, 8, 128),
        vmem(CHUNKS, NS, L3, 8, 128),
        pltpu.SemaphoreType.DMA((6,)),
        pltpu.SemaphoreType.DMA((12,)),
        pltpu.SemaphoreType.DMA((12,)),
        pltpu.SemaphoreType.DMA((5,)),
        pltpu.SemaphoreType.DMA((5,)),
    ]
    out = pl.pallas_call(
        body,
        out_shape=jax.ShapeDtypeStruct((1024, 128), F32),
        in_specs=[pl.BlockSpec(memory_space=pltpu.HBM)] * 6,
        out_specs=pl.BlockSpec(memory_space=pltpu.VMEM),
        scratch_shapes=scratch,
        compiler_params=pltpu.CompilerParams(
            collective_id=0, has_side_effects=True, vmem_limit_bytes=53 * 2**20
        ),
        name="propagate",
    )(*operands)
    return out.reshape(8, 2, 16, 2, 2, 128).transpose(0, 1, 2, 4, 3, 5).reshape(shape)


def solution(mesh):
    in_specs = (P("pencil", None, None, "slab", None), P(), P("slab", "pencil"), P(), P(), P())
    out_specs = P("pencil", None, None, "slab", None)
    return jax.shard_map(
        on_device, mesh=mesh, in_specs=in_specs, out_specs=out_specs, check_vma=False
    )
```

```python
import jax
import jax.numpy as jnp
from jax import lax
from jax.experimental import pallas as pl
from jax.experimental.pallas import tpu as pltpu
from jax.sharding import PartitionSpec as P


MESH = pl.DeviceIdType.MESH
F32 = jnp.float32
BF16 = jnp.bfloat16
STEP = 0.1
GRID = 0.5
CHARGE = 3.0
BAND = 0.3
NP = 32
NS = 16
L2 = 8
L3 = 2
C = 16
N = 256
CHUNKS = 2


def iota(shape, dim):
    return lax.broadcasted_iota(jnp.int32, shape, dim)


def split2(x):
    high = x.astype(BF16)
    return high, (x - high.astype(F32)).astype(BF16)


def split3(x):
    high = x.astype(BF16)
    rest = x - high.astype(F32)
    middle = rest.astype(BF16)
    return high, middle, (rest - middle.astype(F32)).astype(BF16)


def product(a, b, contract=((1,), (0,))):
    def one(x, y):
        return lax.dot_general(x, y, (contract, ((), ())), preferred_element_type=F32)

    return one(a[0], b[0]) + (one(a[0], b[1]) + one(a[1], b[0]))


def column(row, count):
    shape = (count, row.shape[1])
    return jnp.sum(jnp.where(iota(shape, 0) == iota(shape, 1), row, jnp.zeros_like(row)), axis=1, keepdims=True)


def radial(position, weight):
    radius = GRID * (position.astype(F32) + 1.0)
    return -CHARGE / radius + weight / (radius * radius)


def flip_blocks(x):
    row, group = iota((1, 8, 128), 1), iota((1, 8, 128), 2) // 16
    for bit in (4, 2, 1):
        lanes = 16 * bit
        has_row, has_group = (row // bit) % 2, (group // bit) % 2
        down = pltpu.roll(pltpu.roll(x, bit, 1), 128 - lanes, 2)
        if bit == 4:
            up = down
        else:
            up = pltpu.roll(pltpu.roll(x, 8 - bit, 1), lanes, 2)
        x = jnp.where(has_row == has_group, x, jnp.where(has_row == 1, down, up))
    return x


def band(x):
    zero = jnp.zeros((2,) + x.shape[1:], F32)
    y = jnp.concatenate([zero, x, zero], axis=0)
    return (BAND / 24.0) * (y[:32] + y[4:36] - 16.0 * (y[1:33] + y[3:35]) + 30.0 * x)


def body(
    x_hbm,
    prop_hbm,
    len_hbm,
    cent_hbm,
    pair_hbm,
    str_hbm,
    o_ref,
    x_ref,
    prop_ref,
    len_ref,
    cent_ref,
    pair_ref,
    str_ref,
    cos_a,
    sin_a,
    wl_a,
    lv_a,
    kron_hi,
    kron_lo,
    mix,
    w1_hi,
    w1_lo,
    q2_hi,
    q2_lo,
    wf_hi,
    wf_lo,
    cos_d,
    sin_d,
    u_hi,
    u_lo,
    len_col,
    len_in,
    len_out,
    ybuf,
    bbuf,
    sbuf,
    dbuf,
    ebuf,
    hbuf,
    gbuf,
    rbuf,
    cos_e,
    sin_e,
    wt_e,
    lv_e,
    len_row,
    edge_in,
    edge_out,
    e_ybuf,
    e_cbuf,
    e_kbuf,
    e_bbuf,
    e_gbuf,
    e_hbuf,
    e_fbuf,
    e_rbuf,
    in_sem,
    send_sem,
    recv_sem,
    len_send,
    len_recv,
):
    p = lax.axis_index("pencil")
    s = lax.axis_index("slab")
    barrier = pltpu.get_barrier_semaphore()

    def far(n, size):
        half = (n + 1) // 2
        return size // 2 + (1 - 2 * (n % 2)) * half

    def pencil_peer(n):
        return lax.rem(p + far(n, NP), NP)

    def slab_peer(n):
        return lax.rem(s + far(n, NS), NS)

    @pl.loop(0, NP - 1)
    def _(n):
        pl.semaphore_signal(barrier, inc=1, device_id=(s, pencil_peer(n)), device_id_type=MESH)

    @pl.loop(0, NS - 1)
    def _(n):
        pl.semaphore_signal(barrier, inc=1, device_id=(slab_peer(n), p), device_id_type=MESH)

    pairs = [
        (pair_hbm, pair_ref),
        (str_hbm, str_ref),
        (cent_hbm, cent_ref),
        (len_hbm, len_ref),
        (x_hbm, x_ref),
        (prop_hbm, prop_ref),
    ]
    inputs = [pltpu.make_async_copy(src, dst, in_sem.at[i]) for i, (src, dst) in enumerate(pairs)]
    for item in inputs:
        item.start()

    def copy(src, dst, k, device):
        return pltpu.make_async_remote_copy(
            src_ref=src,
            dst_ref=dst,
            send_sem=send_sem.at[k],
            recv_sem=recv_sem.at[k],
            device_id=device,
            device_id_type=MESH,
        )

    def pencil_exchange(src, dst, chunk, k):
        @pl.loop(0, NP - 1)
        def _(n):
            q = pencil_peer(n)
            copy(src.at[chunk, q], dst.at[chunk, p], k, (s, q)).start()

        dst[chunk, pl.ds(p, 1)] = src[chunk, pl.ds(p, 1)]

    def slab_exchange(src, dst, chunk, k):
        @pl.loop(0, NS - 1)
        def _(n):
            q = slab_peer(n)
            copy(src.at[chunk, q], dst.at[chunk, s], k, (q, p)).start()

        dst[chunk, pl.ds(s, 1)] = src[chunk, pl.ds(s, 1)]

    def arrived(buf, chunk, k, count):
        part = buf.at[chunk, pl.ds(0, count - 1)]
        copy(part, part, k, (s, p)).wait_recv()

    def left(buf, chunk, k, count):
        part = buf.at[chunk, pl.ds(0, count - 1)]
        copy(part, part, k, (s, p)).wait_send()

    inputs[0].wait()
    inputs[1].wait()
    strength = str_ref[...]
    first, second = pair_ref[0:1, :], pair_ref[1:2, :]

    def hot_rows(labels):
        return (iota((N, 32), 0) % C == labels).astype(F32)

    def hot_cols(labels):
        shape = (32, 32)
        col = jnp.sum(jnp.where(iota(shape, 0) == iota(shape, 1), labels, 0), axis=1, keepdims=True)
        return (iota((32, N), 1) % C == col).astype(F32)

    rows_1, rows_2, cols_1, cols_2 = hot_rows(first), hot_rows(second), hot_cols(first), hot_cols(second)
    tiled = jnp.zeros((N, N), F32)
    for part in split3(strength):
        scale = part.astype(F32)
        tiled = tiled + jnp.dot((rows_1 * scale).astype(BF16), cols_2.astype(BF16), preferred_element_type=F32)
        tiled = tiled + jnp.dot((rows_2 * scale).astype(BF16), cols_1.astype(BF16), preferred_element_type=F32)
    row, col = iota((N, N), 0), iota((N, N), 1)
    kron_hi[...], kron_lo[...] = split2(jnp.where(row // C == col // C, tiled, 0.0))
    row, col = iota((128, 128), 0), iota((128, 128), 1)
    same = (row // C) % 4 == (col // C) % 4
    sign = (row // 64 - col // 64).astype(F32)
    high, low = split2(jnp.where(same, tiled[:128, :128] * sign, 0.0))
    mix[:128, :128], mix[:128, 128:] = high, low
    mix[128:, :128], mix[128:, 128:] = high, jnp.zeros_like(low)

    inputs[2].wait()
    inputs[3].wait()
    half = 0.5 * STEP
    cent = cent_ref[...]
    cent_col = [column(cent[e : e + 1], C) for e in range(3)]
    angle_1 = half * radial(iota((C, N), 1), cent_col[0])
    cos_1, sin_1 = jnp.cos(angle_1), jnp.sin(angle_1)
    lane = iota((C, 16), 1)
    angle_23 = half * (radial(L2 * p + lane % L2, cent_col[1]) + radial(L3 * s + lane // L2, cent_col[2]))
    cos_23, sin_23 = jnp.cos(angle_23), jnp.sin(angle_23)
    for m in range(16):
        c23, s23 = cos_23[:, m : m + 1], sin_23[:, m : m + 1]
        cos_a[m * C : (m + 1) * C] = cos_1 * c23 - sin_1 * s23
        sin_a[m * C : (m + 1) * C] = sin_1 * c23 + cos_1 * s23

    lens = len_ref[...].astype(F32)
    lane = iota((8, 128), 1)
    len_tile = jnp.zeros((8, 128), F32)
    len_rows = []
    for i3 in range(L3):
        col = column(lens[i3 : i3 + 1], L2)
        len_rows.append(col)
        edge_out[i3] = jnp.where(lane == p, col, jnp.zeros_like(col))
        len_tile = len_tile + jnp.where(lane == L3 * s + i3, col, jnp.zeros_like(col))
    len_out[0] = len_tile
    len_a = jnp.concatenate(len_rows, axis=0)

    row, col = iota((16, N), 0), iota((16, N), 1)
    farthest = jnp.maximum(jnp.maximum(L2 * p + row % L2, L3 * s + row // L2), col).astype(F32)
    live = (col.astype(F32) < len_a).astype(F32)
    lv_a[...] = live
    wl_a[...] = live * (half / (1.0 + 0.02 * farthest))

    inputs[4].wait()
    kron = (kron_hi[...], kron_lo[...])

    def coupled(kron, turned):
        high, low = split2(turned)
        if kron[0].shape[1] == N:
            return product(kron, (high, low))
        top = jnp.concatenate([high, low], axis=1)
        bottom = jnp.concatenate([high, jnp.zeros_like(low)], axis=1)
        left_side = jnp.concatenate(kron, axis=1)
        both = jnp.dot(left_side, jnp.concatenate([top, bottom], axis=0), preferred_element_type=F32)
        return both[:, :N] + both[:, N:]

    def potential(re, im, kron, start, count):
        rows_of = slice(start * C, (start + count) * C)
        cosine, sine = cos_a[rows_of], sin_a[rows_of]
        turned_re = re * cosine + im * sine
        turned_im = im * cosine - re * sine
        mixed_re = coupled(kron, turned_im)
        mixed_im = coupled(kron, turned_re)

        def rows(a):
            return jnp.concatenate([jnp.broadcast_to(a[m : m + 1], (C, N)) for m in range(start, start + count)], axis=0)

        weight, alive = rows(wl_a[...]), rows(lv_a[...])
        return turned_re * alive + weight * mixed_re, turned_im * alive - weight * mixed_im

    def load(part):
        blocks = []
        for i3 in range(L3):
            for i2 in range(L2):
                base = (i2 * 2 + part) * 64 + i3
                blocks.append(
                    jnp.concatenate([x_ref[pl.ds(base + 2 * l, C, stride=4), :] for l in range(2)], axis=1)
                )
        return jnp.concatenate(blocks, axis=0)

    v_re, v_im = potential(load(0), load(1), kron, 0, 16)
    u_hi[...], u_lo[...] = split2(jnp.concatenate([v_re, v_im], axis=1))
    u = (u_hi[...], u_lo[...])

    inputs[5].wait()
    sub = iota((1, 8, 2 * N), 1)

    def interleaved(re, im):
        top = jnp.concatenate([re, -im], axis=1).reshape(NP, 8, 2 * N)
        low = jnp.concatenate([im, re], axis=1).reshape(NP, 8, 2 * N)
        early = jnp.where(sub < 4, top, pltpu.roll(low, 4, 1))
        late = jnp.where(sub < 4, pltpu.roll(top, 4, 1), low)
        return [split2(v.reshape(N, 2 * N)) for v in (early, late)]

    for part, (high, low) in enumerate(interleaved(prop_ref[0], prop_ref[1])):
        w1_hi[part], w1_lo[part] = high, low

    def first_line(half_of):
        y = product((w1_hi[half_of], w1_lo[half_of]), u, ((1,), (1,)))
        return [y[:, i * 128 : (i + 1) * 128] for i in range(L3)]

    y = first_line(0)
    for i3 in range(L3):
        ybuf[0, :, i3] = y[i3].reshape(NP, 8, 128)

    root = s == p // 2

    def len_copy(src, dst, k, device):
        return pltpu.make_async_remote_copy(
            src_ref=src,
            dst_ref=dst,
            send_sem=len_send.at[k],
            recv_sem=len_recv.at[k],
            device_id=device,
            device_id_type=MESH,
        )

    y = first_line(1)
    for chunk in range(CHUNKS):
        for i3 in range(L3):
            e_ybuf[chunk, :, i3] = y[i3].reshape(NS, CHUNKS, 8, 128)[:, chunk]

    pl.semaphore_wait(barrier, NP + NS - 2)

    @pl.when(jnp.logical_not(root))
    def _():
        len_copy(len_out.at[0], len_col.at[s], 0, (p // 2, p)).start()

    for i3 in range(L3):

        @pl.when(p != L3 * s + i3)
        def _():
            len_copy(edge_out.at[i3], len_row.at[p], 2 + i3, (s, L3 * s + i3)).start()

    pencil_exchange(ybuf, bbuf, 0, 0)

    for chunk in range(CHUNKS):
        slab_exchange(e_ybuf, e_cbuf, chunk, 4 + chunk)

    @pl.when(root)
    def _():
        len_col[pl.ds(s, 1)] = len_out[pl.ds(0, 1)]
        part = len_col.at[pl.ds(0, NS - 1)]
        len_copy(part, part, 0, (s, p)).wait_recv()
        total = jnp.sum(len_col[...], axis=0)
        len_out[1] = total
        len_in[pl.ds(lax.rem(p, 2), 1)] = total[None]

        @pl.loop(0, NP - 1)
        def _(n):
            len_copy(len_out.at[1], len_in.at[lax.rem(p, 2)], 1, (s, pencil_peer(n))).start()

    def edge_third(x):
        g1 = band(x)
        g2 = band(g1)
        sign = jnp.where(iota((1, 8, 128), 1) < 4, 1.0, -1.0)
        return x + sign * pltpu.roll(g1, 4, 1) - 0.5 * g2

    def edge_1(chunk):
        arrived(e_cbuf, chunk, 4 + chunk, NS)
        e_kbuf[chunk] = edge_third(e_cbuf[chunk].reshape(NP, 8, 128))
        pencil_exchange(e_kbuf, e_bbuf, chunk, 6 + chunk)

    re, im = prop_ref[0], prop_ref[1]
    q2_hi[...], q2_lo[...] = split2(jnp.concatenate([re, im], axis=0))

    edge_1(0)
    edge_1(1)

    @pl.when(root)
    def _():
        len_row[pl.ds(p, 1)] = edge_out[pl.ds(lax.rem(p, 2), 1)]
        part = len_row.at[pl.ds(0, NP - 1)]
        len_copy(part, part, 2 + lax.rem(p, 2), (s, p)).wait_recv()
        total = jnp.sum(len_row[...], axis=0)
        edge_out[2] = total
        edge_in[0] = total

        @pl.loop(0, NS - 1)
        def _(n):
            len_copy(edge_out.at[2], edge_in.at[0], 4, (slab_peer(n), p)).start()

    for part, (high, low) in enumerate(interleaved(re.T, -im.T)):
        wf_hi[part], wf_lo[part] = high, low

    lane = iota((C, 128), 1)
    cent_row = [
        jnp.sum(jnp.where(iota((C, 128), 0) == lane % C, col, 0.0), axis=0, keepdims=True) for col in cent_col
    ]
    lane = iota((1, 128), 1)
    second_pos = 16 * s + iota((16, 128), 0)
    third_pos = iota((32, 128), 0)
    first_pos = 8 * p + (lane // C) % 4

    angle_2 = STEP * radial(second_pos, cent_row[1])
    angle_3 = STEP * radial(third_pos, cent_row[2])
    cos_3, sin_3 = jnp.cos(angle_3), jnp.sin(angle_3)
    turn = jnp.where(lane < 64, 1.0, -1.0)
    angle_12 = angle_2 + STEP * radial(first_pos, cent_row[0])
    cos_12, sin_12 = jnp.cos(angle_12), jnp.sin(angle_12)
    for i in range(32):
        c3, s3 = cos_3[i : i + 1], sin_3[i : i + 1]
        cos_d[i] = cos_12 * c3 - sin_12 * s3
        sin_d[i] = turn * (sin_12 * c3 + cos_12 * s3)

    angle_2 = STEP * radial(iota((N, 128), 0), cent_row[1])
    cos_2, sin_2 = jnp.cos(angle_2), jnp.sin(angle_2)
    edge_rows = iota((N, 128), 0)

    def edge_first_pos(chunk):
        return 8 * (CHUNKS * s + chunk) + 4 + (lane // C) % 4

    for chunk in range(CHUNKS):
        position = edge_first_pos(chunk)
        angle_13 = STEP * (radial(position, cent_row[0]) + radial(jnp.full((1, 128), p, jnp.int32), cent_row[2]))
        cos_13, sin_13 = jnp.cos(angle_13), jnp.sin(angle_13)
        cos_e[chunk] = cos_2 * cos_13 - sin_2 * sin_13
        sin_e[chunk] = turn * (sin_2 * cos_13 + cos_2 * sin_13)
        farthest = jnp.maximum(jnp.maximum(edge_rows, position), p).astype(F32)
        wt_e[chunk] = STEP / (1.0 + 0.02 * farthest)

    q2 = (q2_hi[...], q2_lo[...])

    def second_line(z):
        high, low = split2(z)
        both = jnp.dot(q2[0], jnp.concatenate([high, low], axis=1), preferred_element_type=F32)
        both = both[:, :128] + both[:, 128:] + jnp.dot(q2[1], high, preferred_element_type=F32)
        return both[:N] - turn * pltpu.roll(both[N:], 64, 1)

    def mixture(turned):
        both = jnp.dot(jnp.concatenate(split2(turned), axis=1), mix[...], preferred_element_type=F32)
        return both[:, :128] + both[:, 128:]

    def third_line(psi):
        g1 = band(psi)
        g2 = band(g1)
        return psi + turn * pltpu.roll(g1, 64, 2) - 0.5 * g2

    def third_potential(psi):
        turned = psi * cos_d[...] + sin_d[...] * pltpu.roll(psi, 64, 2)
        mixed = mixture(turned.reshape(512, 128)).reshape(32, 16, 128)
        both = jnp.maximum(second_pos, first_pos)
        lengths = jnp.concatenate([len_in[0], len_in[1]], axis=0)
        out = []
        for i in range(32):
            weight = STEP / (1.0 + 0.02 * jnp.maximum(both, i).astype(F32))
            alive = first_pos.astype(F32) < lengths[:, i : i + 1]
            out.append(jnp.where(alive, turned[i] + weight * mixed[i], 0.0))
        return jnp.stack(out, axis=0)

    def second_pair(z):
        both = product(q2, split2(jnp.concatenate(z, axis=1)))
        both = [both[:, i * 128 : (i + 1) * 128] for i in range(L3)]
        return [b[:N] - turn * pltpu.roll(b[N:], 64, 1) for b in both]

    def step_1():
        arrived(bbuf, 0, 0, NP)
        z = second_pair([flip_blocks(bbuf[0, :, i3]).reshape(N, 128) for i3 in range(L3)])
        for i3 in range(L3):
            sbuf[0, :, i3] = z[i3].reshape(NS, 16, 128)
        slab_exchange(sbuf, dbuf, 0, 1)

    def step_2():
        arrived(dbuf, 0, 1, NS)
        psi = third_line(dbuf[0].reshape(32, 16, 128))
        ebuf[0] = third_line(third_potential(psi)).reshape(NS, L3, 16, 128)
        slab_exchange(ebuf, hbuf, 0, 2)

    def step_3():
        arrived(hbuf, 0, 2, NS)
        z = second_pair([hbuf[0, :, i3].reshape(N, 128) for i3 in range(L3)])
        for i3 in range(L3):
            gbuf[0, :, i3] = flip_blocks(z[i3].reshape(NP, 8, 128))
        pencil_exchange(gbuf, rbuf, 0, 3)

    def edge_potential(psi, chunk):
        turned = psi * cos_e[chunk] + sin_e[chunk] * pltpu.roll(psi, 64, 1)
        mixed = mixture(turned)
        return lv_e[chunk] * turned + wt_e[chunk] * mixed

    def edge_2(chunk):
        arrived(e_bbuf, chunk, 6 + chunk, NP)
        z = second_line(flip_blocks(e_bbuf[chunk]).reshape(N, 128))
        z = second_line(edge_potential(z, chunk))
        e_gbuf[chunk] = flip_blocks(z.reshape(NP, 8, 128))
        pencil_exchange(e_gbuf, e_hbuf, chunk, 8 + chunk)

    def edge_3(chunk):
        arrived(e_hbuf, chunk, 8 + chunk, NP)
        e_fbuf[chunk] = edge_third(e_hbuf[chunk]).reshape(NS, L3, 8, 128)
        slab_exchange(e_fbuf, e_rbuf, chunk, 10 + chunk)

    step_1()

    @pl.when(root)
    def _():
        len_copy(len_in.at[0], len_in.at[0], 1, (s, p)).wait_recv()

    @pl.when(jnp.logical_not(root))
    def _():
        len_copy(len_in, len_in, 1, (s, p)).wait_recv()
        len_copy(edge_in, edge_in, 4, (s, p)).wait_recv()

    lengths = edge_in[0]
    end = jnp.concatenate([jnp.broadcast_to(lengths[:, i : i + 1], (8, 128)) for i in range(NP)], axis=0)
    for chunk in range(CHUNKS):
        alive = (edge_first_pos(chunk).astype(F32) < end).astype(F32)
        lv_e[chunk] = alive
        wt_e[chunk] = alive * wt_e[chunk]

    edge_2(0)
    step_2()
    edge_2(1)
    step_3()

    edge_3(0)
    edge_3(1)
    for chunk in range(CHUNKS):
        arrived(e_rbuf, chunk, 10 + chunk, NS)
    r = [jnp.stack([e_rbuf[chunk, :, i3] for chunk in range(CHUNKS)], axis=1).reshape(N, 128) for i3 in range(L3)]
    wf = [(wf_hi[k], wf_lo[k]) for k in range(2)]
    early = [product(split2(a.T), wf[1]) for a in r]
    arrived(rbuf, 0, 3, NP)
    block = (kron_hi[:128, :128], kron_lo[:128, :128])
    for i3 in range(L3):
        out = early[i3] + product(split2(rbuf[0, :, i3].reshape(N, 128).T), wf[0])
        out = potential(out[:, :N], out[:, N:], block, i3 * L2, L2)
        for part in range(2):
            for i2 in range(L2):
                base = (i2 * 2 + part) * 64 + i3
                for l in range(2):
                    o_ref[pl.ds(base + 2 * l, C, stride=4), :] = out[part][i2 * C : (i2 + 1) * C, l * 128 : (l + 1) * 128]

    left(ybuf, 0, 0, NP)
    left(sbuf, 0, 1, NS)
    left(ebuf, 0, 2, NS)
    left(gbuf, 0, 3, NP)
    for chunk in range(CHUNKS):
        left(e_ybuf, chunk, 4 + chunk, NS)
        left(e_kbuf, chunk, 6 + chunk, NP)
        left(e_gbuf, chunk, 8 + chunk, NP)
        left(e_fbuf, chunk, 10 + chunk, NS)

    @pl.when(root)
    def _():
        @pl.loop(0, NP - 1)
        def _(n):
            len_copy(len_out.at[1], len_in.at[0], 1, (s, p)).wait_send()

        @pl.loop(0, NS - 1)
        def _(n):
            len_copy(edge_out.at[2], edge_in.at[0], 4, (s, p)).wait_send()

    @pl.when(jnp.logical_not(root))
    def _():
        len_copy(len_out.at[0], len_col.at[0], 0, (s, p)).wait_send()

    for i3 in range(L3):

        @pl.when(p != L3 * s + i3)
        def _():
            len_copy(edge_out.at[i3], len_row.at[0], 2 + i3, (s, p)).wait_send()


def on_device(wavefunction, propagator, lengths, centrifugal, channel_pairs, strengths):
    shape = wavefunction.shape
    x = wavefunction.reshape(8, 2, 16, 2, 2, 128).transpose(0, 1, 2, 4, 3, 5).reshape(1024, 128)
    operands = (x, propagator, lengths, centrifugal, channel_pairs.T, strengths.reshape(1, 32))

    def vmem(*dims, dtype=F32):
        return pltpu.VMEM(dims, dtype)

    scratch = [pltpu.VMEM(a.shape, a.dtype) for a in operands]
    scratch += [
        vmem(N, N),
        vmem(N, N),
        vmem(16, N),
        vmem(16, N),
        vmem(N, N, dtype=BF16),
        vmem(N, N, dtype=BF16),
        vmem(N, N, dtype=BF16),
        vmem(2, N, 2 * N, dtype=BF16),
        vmem(2, N, 2 * N, dtype=BF16),
        vmem(2 * N, N, dtype=BF16),
        vmem(2 * N, N, dtype=BF16),
        vmem(2, N, 2 * N, dtype=BF16),
        vmem(2, N, 2 * N, dtype=BF16),
        vmem(32, 16, 128),
        vmem(32, 16, 128),
        vmem(N, 2 * N, dtype=BF16),
        vmem(N, 2 * N, dtype=BF16),
        vmem(NS, 8, 128),
        vmem(2, 8, 128),
        vmem(2, 8, 128),
        vmem(1, NP, L3, 8, 128),
        vmem(1, NP, L3, 8, 128),
        vmem(1, NS, L3, 16, 128),
        vmem(1, NS, L3, 16, 128),
        vmem(1, NS, L3, 16, 128),
        vmem(1, NS, L3, 16, 128),
        vmem(1, NP, L3, 8, 128),
        vmem(1, NP, L3, 8, 128),
        vmem(CHUNKS, N, 128),
        vmem(CHUNKS, N, 128),
        vmem(CHUNKS, N, 128),
        vmem(CHUNKS, N, 128),
        vmem(NP, 8, 128),
        vmem(1, 8, 128),
        vmem(3, 8, 128),
        vmem(CHUNKS, NS, L3, 8, 128),
        vmem(CHUNKS, NS, L3, 8, 128),
        vmem(CHUNKS, NP, 8, 128),
        vmem(CHUNKS, NP, 8, 128),
        vmem(CHUNKS, NP, 8, 128),
        vmem(CHUNKS, NP, 8, 128),
        vmem(CHUNKS, NS, L3, 8, 128),
        vmem(CHUNKS, NS, L3, 8, 128),
        pltpu.SemaphoreType.DMA((6,)),
        pltpu.SemaphoreType.DMA((12,)),
        pltpu.SemaphoreType.DMA((12,)),
        pltpu.SemaphoreType.DMA((5,)),
        pltpu.SemaphoreType.DMA((5,)),
    ]
    out = pl.pallas_call(
        body,
        out_shape=jax.ShapeDtypeStruct((1024, 128), F32),
        in_specs=[pl.BlockSpec(memory_space=pltpu.HBM)] * 6,
        out_specs=pl.BlockSpec(memory_space=pltpu.VMEM),
        scratch_shapes=scratch,
        compiler_params=pltpu.CompilerParams(
            collective_id=0, has_side_effects=True, vmem_limit_bytes=53 * 2**20
        ),
        name="propagate",
    )(*operands)
    return out.reshape(8, 2, 16, 2, 2, 128).transpose(0, 1, 2, 4, 3, 5).reshape(shape)


def solution(mesh):
    in_specs = (P("pencil", None, None, "slab", None), P(), P("slab", "pencil"), P(), P(), P())
    out_specs = P("pencil", None, None, "slab", None)
    return jax.shard_map(
        on_device, mesh=mesh, in_specs=in_specs, out_specs=out_specs, check_vma=False
    )
```

```python
import jax
import jax.numpy as jnp
from jax import lax
from jax.experimental import pallas as pl
from jax.experimental.pallas import tpu as pltpu
from jax.sharding import PartitionSpec as P


MESH = pl.DeviceIdType.MESH
F32 = jnp.float32
BF16 = jnp.bfloat16
STEP = 0.1
GRID = 0.5
CHARGE = 3.0
BAND = 0.3
NP = 32
NS = 16
L2 = 8
L3 = 2
C = 16
N = 256
CHUNKS = 2


def iota(shape, dim):
    return lax.broadcasted_iota(jnp.int32, shape, dim)


def split2(x):
    high = x.astype(BF16)
    return high, (x - high.astype(F32)).astype(BF16)


def split3(x):
    high = x.astype(BF16)
    rest = x - high.astype(F32)
    middle = rest.astype(BF16)
    return high, middle, (rest - middle.astype(F32)).astype(BF16)


def product(a, b, contract=((1,), (0,))):
    def one(x, y):
        return lax.dot_general(x, y, (contract, ((), ())), preferred_element_type=F32)

    return one(a[0], b[0]) + (one(a[0], b[1]) + one(a[1], b[0]))


def column(row, count):
    shape = (count, row.shape[1])
    return jnp.sum(jnp.where(iota(shape, 0) == iota(shape, 1), row, jnp.zeros_like(row)), axis=1, keepdims=True)


def radial(position, weight):
    radius = GRID * (position.astype(F32) + 1.0)
    return -CHARGE / radius + weight / (radius * radius)


def flip_blocks(x):
    row, group = iota((1, 8, 128), 1), iota((1, 8, 128), 2) // 16
    for bit in (4, 2, 1):
        lanes = 16 * bit
        has_row, has_group = (row // bit) % 2, (group // bit) % 2
        down = pltpu.roll(pltpu.roll(x, bit, 1), 128 - lanes, 2)
        if bit == 4:
            up = down
        else:
            up = pltpu.roll(pltpu.roll(x, 8 - bit, 1), lanes, 2)
        x = jnp.where(has_row == has_group, x, jnp.where(has_row == 1, down, up))
    return x


def band(x):
    zero = jnp.zeros((2,) + x.shape[1:], F32)
    y = jnp.concatenate([zero, x, zero], axis=0)
    return (BAND / 24.0) * (y[:32] + y[4:36] - 16.0 * (y[1:33] + y[3:35]) + 30.0 * x)


def body(
    x_hbm,
    prop_hbm,
    len_hbm,
    cent_hbm,
    pair_hbm,
    str_hbm,
    o_ref,
    x_ref,
    prop_ref,
    len_ref,
    cent_ref,
    pair_ref,
    str_ref,
    cos_a,
    sin_a,
    wl_a,
    lv_a,
    kron_hi,
    kron_lo,
    mix,
    w1_hi,
    w1_lo,
    q2_hi,
    q2_lo,
    wf_hi,
    wf_lo,
    cos_d,
    sin_d,
    u_hi,
    u_lo,
    len_col,
    len_in,
    len_out,
    ybuf,
    bbuf,
    sbuf,
    dbuf,
    ebuf,
    hbuf,
    gbuf,
    rbuf,
    cos_e,
    sin_e,
    wt_e,
    len_row,
    edge_in,
    edge_out,
    e_ybuf,
    e_cbuf,
    e_kbuf,
    e_bbuf,
    e_gbuf,
    e_hbuf,
    e_fbuf,
    e_rbuf,
    in_sem,
    send_sem,
    recv_sem,
    len_send,
    len_recv,
):
    p = lax.axis_index("pencil")
    s = lax.axis_index("slab")
    barrier = pltpu.get_barrier_semaphore()

    def far(n, size):
        half = (n + 1) // 2
        return size // 2 + (1 - 2 * (n % 2)) * half

    def pencil_peer(n):
        return lax.rem(p + far(n, NP), NP)

    def slab_peer(n):
        return lax.rem(s + far(n, NS), NS)

    @pl.loop(0, NP - 1)
    def _(n):
        pl.semaphore_signal(barrier, inc=1, device_id=(s, pencil_peer(n)), device_id_type=MESH)

    @pl.loop(0, NS - 1)
    def _(n):
        pl.semaphore_signal(barrier, inc=1, device_id=(slab_peer(n), p), device_id_type=MESH)

    pairs = [
        (pair_hbm, pair_ref),
        (str_hbm, str_ref),
        (cent_hbm, cent_ref),
        (len_hbm, len_ref),
        (x_hbm, x_ref),
        (prop_hbm, prop_ref),
    ]
    inputs = [pltpu.make_async_copy(src, dst, in_sem.at[i]) for i, (src, dst) in enumerate(pairs)]
    for item in inputs:
        item.start()

    def copy(src, dst, k, device):
        return pltpu.make_async_remote_copy(
            src_ref=src,
            dst_ref=dst,
            send_sem=send_sem.at[k],
            recv_sem=recv_sem.at[k],
            device_id=device,
            device_id_type=MESH,
        )

    def pencil_exchange(src, dst, chunk, k):
        @pl.loop(0, NP - 1)
        def _(n):
            q = pencil_peer(n)
            copy(src.at[chunk, q], dst.at[chunk, p], k, (s, q)).start()

        dst[chunk, pl.ds(p, 1)] = src[chunk, pl.ds(p, 1)]

    def slab_exchange(src, dst, chunk, k):
        @pl.loop(0, NS - 1)
        def _(n):
            q = slab_peer(n)
            copy(src.at[chunk, q], dst.at[chunk, s], k, (q, p)).start()

        dst[chunk, pl.ds(s, 1)] = src[chunk, pl.ds(s, 1)]

    def arrived(buf, chunk, k, count):
        part = buf.at[chunk, pl.ds(0, count - 1)]
        copy(part, part, k, (s, p)).wait_recv()

    def left(buf, chunk, k, count):
        part = buf.at[chunk, pl.ds(0, count - 1)]
        copy(part, part, k, (s, p)).wait_send()

    inputs[0].wait()
    inputs[1].wait()
    strength = str_ref[...]
    first, second = pair_ref[0:1, :], pair_ref[1:2, :]

    def hot_rows(labels):
        return (iota((N, 32), 0) % C == labels).astype(F32)

    def hot_cols(labels):
        shape = (32, 32)
        col = jnp.sum(jnp.where(iota(shape, 0) == iota(shape, 1), labels, 0), axis=1, keepdims=True)
        return (iota((32, N), 1) % C == col).astype(F32)

    rows_1, rows_2, cols_1, cols_2 = hot_rows(first), hot_rows(second), hot_cols(first), hot_cols(second)
    tiled = jnp.zeros((N, N), F32)
    for part in split3(strength):
        scale = part.astype(F32)
        tiled = tiled + jnp.dot((rows_1 * scale).astype(BF16), cols_2.astype(BF16), preferred_element_type=F32)
        tiled = tiled + jnp.dot((rows_2 * scale).astype(BF16), cols_1.astype(BF16), preferred_element_type=F32)
    row, col = iota((N, N), 0), iota((N, N), 1)
    kron_hi[...], kron_lo[...] = split2(jnp.where(row // C == col // C, tiled, 0.0))
    row, col = iota((128, 128), 0), iota((128, 128), 1)
    same = (row // C) % 4 == (col // C) % 4
    sign = (row // 64 - col // 64).astype(F32)
    high, low = split2(jnp.where(same, tiled[:128, :128] * sign, 0.0))
    mix[:128, :128], mix[:128, 128:] = high, low
    mix[128:, :128], mix[128:, 128:] = high, jnp.zeros_like(low)

    inputs[2].wait()
    inputs[3].wait()
    half = 0.5 * STEP
    cent = cent_ref[...]
    cent_col = [column(cent[e : e + 1], C) for e in range(3)]
    angle_1 = half * radial(iota((C, N), 1), cent_col[0])
    cos_1, sin_1 = jnp.cos(angle_1), jnp.sin(angle_1)
    lane = iota((C, 16), 1)
    angle_23 = half * (radial(L2 * p + lane % L2, cent_col[1]) + radial(L3 * s + lane // L2, cent_col[2]))
    cos_23, sin_23 = jnp.cos(angle_23), jnp.sin(angle_23)
    for m in range(16):
        c23, s23 = cos_23[:, m : m + 1], sin_23[:, m : m + 1]
        cos_a[m * C : (m + 1) * C] = cos_1 * c23 - sin_1 * s23
        sin_a[m * C : (m + 1) * C] = sin_1 * c23 + cos_1 * s23

    lens = len_ref[...].astype(F32)
    lane = iota((8, 128), 1)
    len_tile = jnp.zeros((8, 128), F32)
    len_rows = []
    for i3 in range(L3):
        col = column(lens[i3 : i3 + 1], L2)
        len_rows.append(col)
        edge_out[i3] = jnp.where(lane == p, col, jnp.zeros_like(col))
        len_tile = len_tile + jnp.where(lane == L3 * s + i3, col, jnp.zeros_like(col))
    len_out[0] = len_tile
    len_a = jnp.concatenate(len_rows, axis=0)

    row, col = iota((16, N), 0), iota((16, N), 1)
    farthest = jnp.maximum(jnp.maximum(L2 * p + row % L2, L3 * s + row // L2), col).astype(F32)
    live = (col.astype(F32) < len_a).astype(F32)
    lv_a[...] = live
    wl_a[...] = live * (half / (1.0 + 0.02 * farthest))

    inputs[4].wait()
    kron = (kron_hi[...], kron_lo[...])

    def potential(re, im, kron, start, count):
        rows_of = slice(start * C, (start + count) * C)
        cosine, sine = cos_a[rows_of], sin_a[rows_of]
        turned_re = re * cosine + im * sine
        turned_im = im * cosine - re * sine
        mixed_re = product(kron, split2(turned_im))
        mixed_im = product(kron, split2(turned_re))

        def rows(a):
            return jnp.concatenate([jnp.broadcast_to(a[m : m + 1], (C, N)) for m in range(start, start + count)], axis=0)

        weight, alive = rows(wl_a[...]), rows(lv_a[...])
        return turned_re * alive + weight * mixed_re, turned_im * alive - weight * mixed_im

    def load(part):
        blocks = []
        for i3 in range(L3):
            for i2 in range(L2):
                base = (i2 * 2 + part) * 64 + i3
                blocks.append(
                    jnp.concatenate([x_ref[pl.ds(base + 2 * l, C, stride=4), :] for l in range(2)], axis=1)
                )
        return jnp.concatenate(blocks, axis=0)

    v_re, v_im = potential(load(0), load(1), kron, 0, 16)
    u_hi[...], u_lo[...] = split2(jnp.concatenate([v_re, v_im], axis=1))
    u = (u_hi[...], u_lo[...])

    inputs[5].wait()
    sub = iota((1, 8, 2 * N), 1)

    def interleaved(re, im):
        top = jnp.concatenate([re, -im], axis=1).reshape(NP, 8, 2 * N)
        low = jnp.concatenate([im, re], axis=1).reshape(NP, 8, 2 * N)
        early = jnp.where(sub < 4, top, pltpu.roll(low, 4, 1))
        late = jnp.where(sub < 4, pltpu.roll(top, 4, 1), low)
        return [split2(v.reshape(N, 2 * N)) for v in (early, late)]

    for part, (high, low) in enumerate(interleaved(prop_ref[0], prop_ref[1])):
        w1_hi[part], w1_lo[part] = high, low

    def first_line(half_of):
        y = product((w1_hi[half_of], w1_lo[half_of]), u, ((1,), (1,)))
        return [y[:, i * 128 : (i + 1) * 128] for i in range(L3)]

    y = first_line(0)
    for i3 in range(L3):
        ybuf[0, :, i3] = y[i3].reshape(NP, 8, 128)

    root = s == p // 2

    def len_copy(src, dst, k, device):
        return pltpu.make_async_remote_copy(
            src_ref=src,
            dst_ref=dst,
            send_sem=len_send.at[k],
            recv_sem=len_recv.at[k],
            device_id=device,
            device_id_type=MESH,
        )

    pl.semaphore_wait(barrier, NP + NS - 2)

    @pl.when(jnp.logical_not(root))
    def _():
        len_copy(len_out.at[0], len_col.at[s], 0, (p // 2, p)).start()

    for i3 in range(L3):

        @pl.when(p != L3 * s + i3)
        def _():
            len_copy(edge_out.at[i3], len_row.at[p], 2 + i3, (s, L3 * s + i3)).start()

    pencil_exchange(ybuf, bbuf, 0, 0)

    y = first_line(1)
    for chunk in range(CHUNKS):
        for i3 in range(L3):
            e_ybuf[chunk, :, i3] = y[i3].reshape(NS, CHUNKS, 8, 128)[:, chunk]
        slab_exchange(e_ybuf, e_cbuf, chunk, 4 + chunk)

    @pl.when(root)
    def _():
        len_col[pl.ds(s, 1)] = len_out[pl.ds(0, 1)]
        part = len_col.at[pl.ds(0, NS - 1)]
        len_copy(part, part, 0, (s, p)).wait_recv()
        total = jnp.sum(len_col[...], axis=0)
        len_out[1] = total
        len_in[pl.ds(lax.rem(p, 2), 1)] = total[None]

        @pl.loop(0, NP - 1)
        def _(n):
            len_copy(len_out.at[1], len_in.at[lax.rem(p, 2)], 1, (s, pencil_peer(n))).start()

    def edge_third(x):
        g1 = band(x)
        g2 = band(g1)
        sign = jnp.where(iota((1, 8, 128), 1) < 4, 1.0, -1.0)
        return x + sign * pltpu.roll(g1, 4, 1) - 0.5 * g2

    def edge_1(chunk):
        arrived(e_cbuf, chunk, 4 + chunk, NS)
        e_kbuf[chunk] = edge_third(e_cbuf[chunk].reshape(NP, 8, 128))
        pencil_exchange(e_kbuf, e_bbuf, chunk, 6 + chunk)

    re, im = prop_ref[0], prop_ref[1]
    q2_hi[...], q2_lo[...] = split2(jnp.concatenate([re, im], axis=0))

    edge_1(0)
    edge_1(1)

    @pl.when(root)
    def _():
        len_row[pl.ds(p, 1)] = edge_out[pl.ds(lax.rem(p, 2), 1)]
        part = len_row.at[pl.ds(0, NP - 1)]
        len_copy(part, part, 2 + lax.rem(p, 2), (s, p)).wait_recv()
        total = jnp.sum(len_row[...], axis=0)
        edge_out[2] = total
        edge_in[0] = total

        @pl.loop(0, NS - 1)
        def _(n):
            len_copy(edge_out.at[2], edge_in.at[0], 4, (slab_peer(n), p)).start()

    for part, (high, low) in enumerate(interleaved(re.T, -im.T)):
        wf_hi[part], wf_lo[part] = high, low

    lane = iota((C, 128), 1)
    cent_row = [
        jnp.sum(jnp.where(iota((C, 128), 0) == lane % C, col, 0.0), axis=0, keepdims=True) for col in cent_col
    ]
    lane = iota((1, 128), 1)
    second_pos = 16 * s + iota((16, 128), 0)
    third_pos = iota((32, 128), 0)
    first_pos = 8 * p + (lane // C) % 4

    angle_2 = STEP * radial(second_pos, cent_row[1])
    angle_3 = STEP * radial(third_pos, cent_row[2])
    cos_3, sin_3 = jnp.cos(angle_3), jnp.sin(angle_3)
    turn = jnp.where(lane < 64, 1.0, -1.0)
    angle_12 = angle_2 + STEP * radial(first_pos, cent_row[0])
    cos_12, sin_12 = jnp.cos(angle_12), jnp.sin(angle_12)
    for i in range(32):
        c3, s3 = cos_3[i : i + 1], sin_3[i : i + 1]
        cos_d[i] = cos_12 * c3 - sin_12 * s3
        sin_d[i] = turn * (sin_12 * c3 + cos_12 * s3)

    angle_2 = STEP * radial(iota((N, 128), 0), cent_row[1])
    cos_2, sin_2 = jnp.cos(angle_2), jnp.sin(angle_2)
    edge_rows = iota((N, 128), 0)

    def edge_first_pos(chunk):
        return 8 * (CHUNKS * s + chunk) + 4 + (lane // C) % 4

    for chunk in range(CHUNKS):
        position = edge_first_pos(chunk)
        angle_13 = STEP * (radial(position, cent_row[0]) + radial(jnp.full((1, 128), p, jnp.int32), cent_row[2]))
        cos_13, sin_13 = jnp.cos(angle_13), jnp.sin(angle_13)
        cos_e[chunk] = cos_2 * cos_13 - sin_2 * sin_13
        sin_e[chunk] = turn * (sin_2 * cos_13 + cos_2 * sin_13)
        farthest = jnp.maximum(jnp.maximum(edge_rows, position), p).astype(F32)
        wt_e[chunk] = STEP / (1.0 + 0.02 * farthest)

    q2 = (q2_hi[...], q2_lo[...])

    def second_line(z):
        high, low = split2(z)
        both = jnp.dot(q2[0], jnp.concatenate([high, low], axis=1), preferred_element_type=F32)
        both = both[:, :128] + both[:, 128:] + jnp.dot(q2[1], high, preferred_element_type=F32)
        return both[:N] - turn * pltpu.roll(both[N:], 64, 1)

    def mixture(turned):
        both = jnp.dot(jnp.concatenate(split2(turned), axis=1), mix[...], preferred_element_type=F32)
        return both[:, :128] + both[:, 128:]

    def third_line(psi):
        g1 = band(psi)
        g2 = band(g1)
        return psi + turn * pltpu.roll(g1, 64, 2) - 0.5 * g2

    def third_potential(psi):
        turned = psi * cos_d[...] + sin_d[...] * pltpu.roll(psi, 64, 2)
        mixed = mixture(turned.reshape(512, 128)).reshape(32, 16, 128)
        both = jnp.maximum(second_pos, first_pos)
        lengths = jnp.concatenate([len_in[0], len_in[1]], axis=0)
        out = []
        for i in range(32):
            weight = STEP / (1.0 + 0.02 * jnp.maximum(both, i).astype(F32))
            alive = first_pos.astype(F32) < lengths[:, i : i + 1]
            out.append(jnp.where(alive, turned[i] + weight * mixed[i], 0.0))
        return jnp.stack(out, axis=0)

    def second_pair(z):
        both = product(q2, split2(jnp.concatenate(z, axis=1)))
        both = [both[:, i * 128 : (i + 1) * 128] for i in range(L3)]
        return [b[:N] - turn * pltpu.roll(b[N:], 64, 1) for b in both]

    def step_1():
        arrived(bbuf, 0, 0, NP)
        z = second_pair([flip_blocks(bbuf[0, :, i3]).reshape(N, 128) for i3 in range(L3)])
        for i3 in range(L3):
            sbuf[0, :, i3] = z[i3].reshape(NS, 16, 128)
        slab_exchange(sbuf, dbuf, 0, 1)

    def step_2():
        arrived(dbuf, 0, 1, NS)
        psi = third_line(dbuf[0].reshape(32, 16, 128))
        ebuf[0] = third_line(third_potential(psi)).reshape(NS, L3, 16, 128)
        slab_exchange(ebuf, hbuf, 0, 2)

    def step_3():
        arrived(hbuf, 0, 2, NS)
        z = second_pair([hbuf[0, :, i3].reshape(N, 128) for i3 in range(L3)])
        for i3 in range(L3):
            gbuf[i3] = flip_blocks(z[i3].reshape(NP, 8, 128))
            pencil_exchange(gbuf, rbuf, i3, 3 + 9 * i3)

    def edge_potential(psi, chunk):
        turned = psi * cos_e[chunk] + sin_e[chunk] * pltpu.roll(psi, 64, 1)
        mixed = mixture(turned)
        lengths = edge_in[0]
        end = jnp.concatenate([jnp.broadcast_to(lengths[:, i : i + 1], (8, 128)) for i in range(NP)], axis=0)
        return jnp.where(edge_first_pos(chunk).astype(F32) < end, turned + wt_e[chunk] * mixed, 0.0)

    def edge_2(chunk):
        arrived(e_bbuf, chunk, 6 + chunk, NP)
        z = second_line(flip_blocks(e_bbuf[chunk]).reshape(N, 128))
        z = second_line(edge_potential(z, chunk))
        e_gbuf[chunk] = flip_blocks(z.reshape(NP, 8, 128))
        pencil_exchange(e_gbuf, e_hbuf, chunk, 8 + chunk)

    def edge_3(chunk):
        arrived(e_hbuf, chunk, 8 + chunk, NP)
        e_fbuf[chunk] = edge_third(e_hbuf[chunk]).reshape(NS, L3, 8, 128)
        slab_exchange(e_fbuf, e_rbuf, chunk, 10 + chunk)

    step_1()

    @pl.when(root)
    def _():
        len_copy(len_in.at[0], len_in.at[0], 1, (s, p)).wait_recv()

    @pl.when(jnp.logical_not(root))
    def _():
        len_copy(len_in, len_in, 1, (s, p)).wait_recv()
        len_copy(edge_in, edge_in, 4, (s, p)).wait_recv()

    edge_2(0)
    step_2()
    edge_2(1)
    step_3()

    edge_3(0)
    edge_3(1)
    for chunk in range(CHUNKS):
        arrived(e_rbuf, chunk, 10 + chunk, NS)
    r = [jnp.stack([e_rbuf[chunk, :, i3] for chunk in range(CHUNKS)], axis=1).reshape(N, 128) for i3 in range(L3)]
    wf = [(wf_hi[k], wf_lo[k]) for k in range(2)]
    early = [product(split2(a.T), wf[1]) for a in r]
    block = (kron_hi[:128, :128], kron_lo[:128, :128])
    for i3 in range(L3):
        arrived(rbuf, i3, 3 + 9 * i3, NP)
        out = early[i3] + product(split2(rbuf[i3].reshape(N, 128).T), wf[0])
        out = potential(out[:, :N], out[:, N:], block, i3 * L2, L2)
        for part in range(2):
            for i2 in range(L2):
                base = (i2 * 2 + part) * 64 + i3
                for l in range(2):
                    o_ref[pl.ds(base + 2 * l, C, stride=4), :] = out[part][i2 * C : (i2 + 1) * C, l * 128 : (l + 1) * 128]

    left(ybuf, 0, 0, NP)
    left(sbuf, 0, 1, NS)
    left(ebuf, 0, 2, NS)
    left(gbuf, 0, 3, NP)
    left(gbuf, 1, 12, NP)
    for chunk in range(CHUNKS):
        left(e_ybuf, chunk, 4 + chunk, NS)
        left(e_kbuf, chunk, 6 + chunk, NP)
        left(e_gbuf, chunk, 8 + chunk, NP)
        left(e_fbuf, chunk, 10 + chunk, NS)

    @pl.when(root)
    def _():
        @pl.loop(0, NP - 1)
        def _(n):
            len_copy(len_out.at[1], len_in.at[0], 1, (s, p)).wait_send()

        @pl.loop(0, NS - 1)
        def _(n):
            len_copy(edge_out.at[2], edge_in.at[0], 4, (s, p)).wait_send()

    @pl.when(jnp.logical_not(root))
    def _():
        len_copy(len_out.at[0], len_col.at[0], 0, (s, p)).wait_send()

    for i3 in range(L3):

        @pl.when(p != L3 * s + i3)
        def _():
            len_copy(edge_out.at[i3], len_row.at[0], 2 + i3, (s, p)).wait_send()


def on_device(wavefunction, propagator, lengths, centrifugal, channel_pairs, strengths):
    shape = wavefunction.shape
    x = wavefunction.reshape(8, 2, 16, 2, 2, 128).transpose(0, 1, 2, 4, 3, 5).reshape(1024, 128)
    operands = (x, propagator, lengths, centrifugal, channel_pairs.T, strengths.reshape(1, 32))

    def vmem(*dims, dtype=F32):
        return pltpu.VMEM(dims, dtype)

    scratch = [pltpu.VMEM(a.shape, a.dtype) for a in operands]
    scratch += [
        vmem(N, N),
        vmem(N, N),
        vmem(16, N),
        vmem(16, N),
        vmem(N, N, dtype=BF16),
        vmem(N, N, dtype=BF16),
        vmem(N, N, dtype=BF16),
        vmem(2, N, 2 * N, dtype=BF16),
        vmem(2, N, 2 * N, dtype=BF16),
        vmem(2 * N, N, dtype=BF16),
        vmem(2 * N, N, dtype=BF16),
        vmem(2, N, 2 * N, dtype=BF16),
        vmem(2, N, 2 * N, dtype=BF16),
        vmem(32, 16, 128),
        vmem(32, 16, 128),
        vmem(N, 2 * N, dtype=BF16),
        vmem(N, 2 * N, dtype=BF16),
        vmem(NS, 8, 128),
        vmem(2, 8, 128),
        vmem(2, 8, 128),
        vmem(1, NP, L3, 8, 128),
        vmem(1, NP, L3, 8, 128),
        vmem(1, NS, L3, 16, 128),
        vmem(1, NS, L3, 16, 128),
        vmem(1, NS, L3, 16, 128),
        vmem(1, NS, L3, 16, 128),
        vmem(L3, NP, 8, 128),
        vmem(L3, NP, 8, 128),
        vmem(CHUNKS, N, 128),
        vmem(CHUNKS, N, 128),
        vmem(CHUNKS, N, 128),
        vmem(NP, 8, 128),
        vmem(1, 8, 128),
        vmem(3, 8, 128),
        vmem(CHUNKS, NS, L3, 8, 128),
        vmem(CHUNKS, NS, L3, 8, 128),
        vmem(CHUNKS, NP, 8, 128),
        vmem(CHUNKS, NP, 8, 128),
        vmem(CHUNKS, NP, 8, 128),
        vmem(CHUNKS, NP, 8, 128),
        vmem(CHUNKS, NS, L3, 8, 128),
        vmem(CHUNKS, NS, L3, 8, 128),
        pltpu.SemaphoreType.DMA((6,)),
        pltpu.SemaphoreType.DMA((13,)),
        pltpu.SemaphoreType.DMA((13,)),
        pltpu.SemaphoreType.DMA((5,)),
        pltpu.SemaphoreType.DMA((5,)),
    ]
    out = pl.pallas_call(
        body,
        out_shape=jax.ShapeDtypeStruct((1024, 128), F32),
        in_specs=[pl.BlockSpec(memory_space=pltpu.HBM)] * 6,
        out_specs=pl.BlockSpec(memory_space=pltpu.VMEM),
        scratch_shapes=scratch,
        compiler_params=pltpu.CompilerParams(
            collective_id=0, has_side_effects=True, vmem_limit_bytes=53 * 2**20
        ),
        name="propagate",
    )(*operands)
    return out.reshape(8, 2, 16, 2, 2, 128).transpose(0, 1, 2, 4, 3, 5).reshape(shape)


def solution(mesh):
    in_specs = (P("pencil", None, None, "slab", None), P(), P("slab", "pencil"), P(), P(), P())
    out_specs = P("pencil", None, None, "slab", None)
    return jax.shard_map(
        on_device, mesh=mesh, in_specs=in_specs, out_specs=out_specs, check_vma=False
    )
```
